128 devices in a mesh: clip: 16 (over y, z), tm: 4 (over x_hi, core), rows: 2 (over x_lo).
Axes of the slice: x: 4 (x_hi: 2, x_lo: 2; x = x_hi * 2 + x_lo), y: 4, z: 4, core: 2. Of those that a mesh axis runs over, the one named last changes fastest.
Arguments:
- inputs: bfloat16 [16, 8, 2, 128, 384], P('clip', 'tm', 'rows'), may hold values from -40 to 40
- cotangent: bfloat16 [16, 8, 2, 128, 384], P('clip', 'tm', 'rows'), may hold values from -6 to 6
- weight: bfloat16 [10368, 384], replicated, may hold values from -0.0625 to 0.0625
- gain: float32 [384], replicated, may hold values from 0.5 to 1.5
- shift_term: float32 [384], replicated, may hold values from -3 to 3
Outputs:
- input_grad: bfloat16 [16, 8, 2, 128, 384], P('clip', 'tm', 'rows')
- weight_grad: float32 [10368, 384], P(('clip', 'tm', 'rows'))
The draws below stay inside these ranges and needn't reach their ends.
All inputs are finite; a program needn't handle non-finite values.
Results may differ from the reference program's by a relative error of at most 0.0004.
The reference program's roundings to bfloat16 on the way (of `active`) count: a program that leaves them out, or rounds other values in their place, can miss the bound.
Values may be sent and summed in bfloat16 or wider, within the bound.
A program may use at most 128 MiB of HBM per device.

```python
import jax
import jax.numpy as jnp
from jax import lax

C = 384
GROUPS = 32
TAPS = 27
WD = 128
CLIPS = 16
NT = 8
NH = 2


def draw_inputs(key, part):
    key_noise, key_cell, key_offset = jax.random.split(key, 3)
    full_shape = (CLIPS, NT, NH, WD, C)
    noise = jnp.clip(jax.random.normal(key_noise, full_shape, jnp.float32), -6.0, 6.0)
    frame_pos = jnp.arange(NT, dtype=jnp.float32).reshape(1, NT, 1, 1, 1)
    rising = 1.0 + 2.0 * frame_pos / (NT - 1)
    cell_scale = jnp.exp(jax.random.uniform(key_cell, (CLIPS, NT, NH, WD, 1), jnp.float32, -0.6, 0.6))
    offset = jax.random.uniform(key_offset, (CLIPS, 1, 1, 1, C), jnp.float32, -1.0, 1.0)
    return (noise * rising * cell_scale + offset).astype(jnp.bfloat16)


def shard_levels(stream_key, shape, cuts, smallest, top_value):
    factor_of = 1.0
    for axis_at, blocks in cuts:
        steps = jax.random.uniform(jax.random.fold_in(jax.random.fold_in(stream_key, 6), axis_at), (blocks,), jnp.float32, smallest / len(cuts), top_value / len(cuts))
        factor_of = factor_of * jnp.repeat(jnp.exp(steps), shape[axis_at] // blocks).reshape((-1,) + (1,) * (len(shape) - 1 - axis_at))
    return factor_of


def centred(stream_key, extent, deviation, limit, cuts=(), held_as=jnp.bfloat16):
    result = jax.random.normal(stream_key, extent, jnp.float32) * deviation
    if len(cuts) > 0:
        result = shard_levels(stream_key, extent, cuts, -0.22, 0.18) * result
    return jnp.clip(result, min=-limit, max=limit).astype(held_as)


def setup_inputs(seed: int = 0) -> dict:
    streams_of = jax.random.split(jax.random.key(seed), 6)
    inputs = draw_inputs(jax.random.fold_in(streams_of[5], 71), 0)
    cotangent = centred(streams_of[1], (CLIPS, NT, NH, WD, C), 1.0, 6.0, ((0, 16), (1, 4), (2, 2)))
    weight = centred(streams_of[2], (TAPS * C, C), (TAPS * C) ** -0.5, 0.0625)
    gain = jnp.clip(jax.random.uniform(streams_of[3], (C,), jnp.float32, 0.5, 1.5), 0.5, 1.5)
    shift_term = centred(streams_of[4], (C,), 0.5, 3.0, (), jnp.float32)
    return {"inputs": inputs, "cotangent": cotangent, "weight": weight, "gain": gain, "shift_term": shift_term}


def group_totals(values):
    return lax.optimization_barrier(jnp.sum(values.reshape(-1, GROUPS, C // GROUPS), axis=(0, 2)))

def spread_groups(stats):
    return jnp.repeat(stats, C // GROUPS)

def reference(inputs, cotangent, weight, gain, shift_term):
    cells_group = NT * NH * WD * (C // GROUPS)
    weight_full = weight.astype(jnp.float32)
    highest = lax.Precision.HIGHEST

    def one_clip(carry, pair):
        signal, upstream = pair
        values = signal.astype(jnp.float32)
        mean_group = group_totals(values) / cells_group
        square_group = group_totals(values * values) / cells_group
        rstd_group = lax.rsqrt(square_group - mean_group * mean_group + 1e-05)
        mean_chan = spread_groups(mean_group)
        rstd_chan = spread_groups(rstd_group)
        normed = (values - mean_chan) * rstd_chan
        shifted = normed * gain + shift_term
        active = jax.nn.silu(shifted).astype(jnp.bfloat16)
        act_pad = jnp.pad(active, ((2, 0), (1, 1), (1, 1), (0, 0))).astype(jnp.float32)
        cot_pad = jnp.pad(upstream, ((0, 2), (1, 1), (1, 1), (0, 0))).astype(jnp.float32)
        cot_rows = upstream.astype(jnp.float32).reshape(-1, C)
        grad_active = jnp.zeros((NT * NH * WD, C), jnp.float32)
        pieces = []
        for tap_t in range(3):
            for tap_h in range(3):
                for tap_w in range(3):
                    index = (tap_t * 3 + tap_h) * 3 + tap_w
                    block = weight_full[index * C:(index + 1) * C]
                    window = act_pad[tap_t:tap_t + NT, tap_h:tap_h + NH, tap_w:tap_w + WD].reshape(-1, C)
                    pieces.append(jnp.dot(window.T, cot_rows, precision=highest))
                    mirror = cot_pad[2 - tap_t:2 - tap_t + NT, 2 - tap_h:2 - tap_h + NH, 2 - tap_w:2 - tap_w + WD].reshape(-1, C)
                    grad_active = grad_active + jnp.dot(mirror, block.T, precision=highest)
        grad_active = grad_active.reshape(NT, NH, WD, C)
        sigma = jax.nn.sigmoid(shifted)
        grad_normed = grad_active * sigma * (1.0 + shifted * (1.0 - sigma)) * gain
        first_mean = spread_groups(group_totals(grad_normed) / cells_group)
        second_mean = spread_groups(group_totals(grad_normed * normed) / cells_group)
        input_grad = upstream.astype(jnp.float32) + rstd_chan * (grad_normed - first_mean - normed * second_mean)
        return (carry + jnp.concatenate(pieces, 0), input_grad.astype(jnp.bfloat16))
    start_sum = jnp.zeros((TAPS * C, C), jnp.float32)
    summed, input_grad = lax.scan(one_clip, start_sum, (inputs, cotangent))
    return (input_grad, summed / (CLIPS * NT))
```

```python
import jax
import jax.numpy as jnp
from jax import lax
from jax.experimental import pallas as pl
from jax.experimental.pallas import tpu as pltpu
from jax.sharding import PartitionSpec as P

MESH = pl.DeviceIdType.MESH
C = 384
SL = 48
PG = 12
POS = 1024
OWN = 256
EPS = 1e-05
CELLS = 12 * 2048
SCALE = 1.0 / 128
WIN1, HOP1, CUT1 = 168, 160, 88
WIN2, HOP2, CUT2 = 48, 40, 24
HALF = 648


def kernel(
    x_hbm, cot_hbm, w_hbm, gain_ref, shift_ref, ig_ref, wg_ref,
    x_own, x_send, x_all, cot, wv, gb, stat, normed_s, dsil_s, lcat, part,
    ig_send, ig_recv, d2m, d2p, bufm, bufp, res1, e2m, e2p, cufm, cufp, res2, fin,
    loc_sem, cs_send, cs_recv, xs_send, xs_recv, is_send, is_recv, r_send, r_recv, f_send, f_recv,
):
    clip, tm, rows = lax.axis_index("clip"), lax.axis_index("tm"), lax.axis_index("rows")
    x_hi, core = tm // 2, tm % 2
    j = tm * 2 + rows
    yy, zz = clip // 4, clip % 4

    def dev(tm_, rows_):
        return (clip, tm_, rows_)

    def ring(tm_, rows_, step):
        hi, co = tm_ // 2, tm_ % 2
        x = (hi * 2 + rows_ + step + 4) % 4
        return (x // 2) * 2 + co, x % 2

    rt, rr = ring(tm, rows, 1)
    lt, lr = ring(tm, rows, -1)
    ot, orow = ring(tm, rows, 2)
    sib_tm = x_hi * 2 + (1 - core)

    x_in = pltpu.make_async_copy(x_hbm, x_own, loc_sem.at[0])
    x_in.start()
    own_slot = pl.ds(pl.multiple_of(tm * OWN, OWN), OWN)
    c_in = pltpu.make_async_copy(cot_hbm, cot.at[rows, own_slot], loc_sem.at[1])
    c_in.start()
    w_in = pltpu.make_async_copy(
        w_hbm.at[:, pl.ds(pl.multiple_of(j * SL, SL), SL)], wv, loc_sem.at[2]
    )
    w_in.start()

    yp, ym = ((yy + 1) % 4) * 4 + zz, ((yy + 3) % 4) * 4 + zz
    zp, zm = yy * 4 + (zz + 1) % 4, yy * 4 + (zz + 3) % 4
    barrier = pltpu.get_barrier_semaphore()
    for k in range(1, 8):
        p = (j + k) % 8
        pl.semaphore_signal(barrier, inc=1, device_id=dev(p // 2, p % 2), device_id_type=MESH)
    for other in (yp, ym, zp, zm):
        pl.semaphore_signal(barrier, inc=1, device_id=(other, tm, rows), device_id_type=MESH)
    pl.semaphore_wait(barrier, 11)

    def frame(tm_, f):
        return pl.ds(pl.multiple_of(tm_ * OWN + f * 128, 128), 128)

    def cot_copy(slot, src, where, to):
        dst = cot.at[where[0], where[1]]
        return pltpu.make_async_remote_copy(
            src_ref=dst if src is None else src, dst_ref=dst,
            send_sem=cs_send.at[slot], recv_sem=cs_recv.at[slot],
            device_id=dev(*to), device_id_type=MESH,
        )

    right, left, sib = (rt, rr), (lt, lr), (sib_tm, rows)
    sends = []
    for slot, f, to in ((0, 0, right), (2, 1, left), (1, 1, right), (3, 0, left)):
        c = cot_copy(slot, cot_hbm.at[pl.ds(f * 128, 128)], (rows, frame(tm, f)), to)
        c.start()
        sends.append(c)
    c = cot_copy(4, cot_hbm, (rows, own_slot), sib)
    c.start()
    sends.append(c)

    def arrived(slot, where):
        cot_copy(slot, None, where, right).wait_recv()

    cot[0, POS:, :] = jnp.zeros((OWN, C), jnp.bfloat16)
    cot[1, POS:, :] = jnp.zeros((OWN, C), jnp.bfloat16)
    x_in.wait()
    x_send[...] = x_own[...].astype(jnp.float32).T.astype(jnp.bfloat16)
    own_lanes = pl.ds(pl.multiple_of(rows * POS + tm * OWN, OWN), OWN)
    x_self = pltpu.make_async_copy(
        x_send.at[pl.ds(pl.multiple_of(j * SL, SL), SL)], x_all.at[:, own_lanes], loc_sem.at[3]
    )
    x_self.start()
    xs = []
    for k in range(1, 8):
        p = (j + k) % 8
        c = pltpu.make_async_remote_copy(
            src_ref=x_send.at[pl.ds(pl.multiple_of(p * SL, SL), SL)], dst_ref=x_all.at[:, own_lanes],
            send_sem=xs_send.at[k - 1], recv_sem=xs_recv.at[k - 1],
            device_id=dev(p // 2, p % 2), device_id_type=MESH,
        )
        c.start()
        xs.append(c)

    gb[0] = jnp.broadcast_to(gain_ref[...], (128, C)).T
    gb[1] = jnp.broadcast_to(shift_ref[...], (128, C)).T
    mine = pl.ds(pl.multiple_of(j * SL, SL), SL)
    gain_l, shift_l = gb[0, mine, :], gb[1, mine, :]

    arrived(0, (lr, frame(lt, 0)))
    c = cot_copy(5, None, (lr, frame(lt, 0)), right)
    c.start()
    sends.append(c)
    arrived(2, (rr, frame(rt, 1)))
    c = cot_copy(6, None, (rr, frame(rt, 1)), left)
    c.start()
    sends.append(c)

    x_self.wait()
    for c in xs:
        c.wait_recv()

    row_g = lax.broadcasted_iota(jnp.int32, (SL, SL), 0)
    col_g = lax.broadcasted_iota(jnp.int32, (SL, SL), 1)

    def group_of(i):
        return sum((i >= PG * k).astype(jnp.int32) for k in (1, 2, 3))

    same = (group_of(row_g) == group_of(col_g)).astype(jnp.float32)

    def group_mean(values):
        total = jnp.sum(values, axis=1, keepdims=True)
        return jnp.dot(
            same, jnp.broadcast_to(total, (SL, 128)), precision=lax.Precision.HIGHEST,
            preferred_element_type=jnp.float32,
        ) * (1.0 / CELLS)

    s1 = jnp.zeros((SL, 128), jnp.float32)
    s2 = jnp.zeros((SL, 128), jnp.float32)
    for b in range(16):
        v = x_all[:, b * 128:(b + 1) * 128].astype(jnp.float32)
        s1 = s1 + v
        s2 = s2 + v * v
    mean = group_mean(s1)
    rstd = lax.rsqrt(group_mean(s2) - mean * mean + EPS)
    stat[...] = rstd

    lane = lax.broadcasted_iota(jnp.int32, (SL, 128), 1)
    for h in range(2):
        for dt in range(2):
            for dw in range(3):
                r0 = h * 432 + (dt * 3 + dw) * SL
                lcat[r0:r0 + SL, 0:(2 - dt) * 128] = jnp.zeros((SL, (2 - dt) * 128), jnp.bfloat16)
        for t in range(8):
            b = h * 8 + t
            sl = slice(b * 128, (b + 1) * 128)
            v = x_all[:, sl].astype(jnp.float32)
            normed = (v - mean) * rstd
            pre = normed * gain_l + shift_l
            s = 1.0 / (1.0 + jnp.exp(-pre))
            act = pre * s
            normed_s[:, sl] = normed
            dsil_s[:, sl] = s * (1.0 + pre * (1.0 - s)) * gain_l
            before = jnp.where(lane == 0, 0.0, pltpu.roll(act, 1, 1))
            after = jnp.where(lane == 127, 0.0, pltpu.roll(act, 127, 1))
            for dw, a in ((0, before), (1, act), (2, after)):
                a = a.astype(jnp.bfloat16)
                for dt in range(3):
                    t_out = t + 2 - dt
                    if t_out < 8:
                        r0 = h * 432 + (dt * 3 + dw) * SL
                        lcat[r0:r0 + SL, t_out * 128:(t_out + 1) * 128] = a

    arrived(1, (lr, frame(lt, 1)))
    arrived(3, (rr, frame(rt, 0)))
    for slot, who in ((7, (lt, lr)), (8, (rt, rr))):
        c = cot_copy(slot, None, (who[1], pl.ds(pl.multiple_of(who[0] * OWN, OWN), OWN)), sib)
        c.start()
        sends.append(c)
    arrived(5, (orow, frame(ot, 0)))
    arrived(6, (orow, frame(ot, 1)))
    c = cot_copy(9, None, (orow, pl.ds(pl.multiple_of(ot * OWN, OWN), OWN)), sib)
    c.start()
    sends.append(c)
    c_in.wait()

    def sib_of(who):
        t_ = who[0]
        return pl.ds(pl.multiple_of(((t_ // 2) * 2 + 1 - t_ % 2) * OWN, OWN), OWN)

    arrived(4, (rows, sib_of((tm, rows))))
    arrived(7, (lr, sib_of((lt, lr))))
    arrived(8, (rr, sib_of((rt, rr))))
    arrived(9, (orow, sib_of((ot, orow))))

    r_0 = jnp.dot(lcat[...], cot[0, 0:POS, :], preferred_element_type=jnp.float32)
    part[432:864] = r_0[0:432]
    part[864:1296] = r_0[432:864]
    r_1 = jnp.dot(lcat[...], cot[1, 0:POS, :], preferred_element_type=jnp.float32)
    part[0:432] = r_1[0:432]
    part[432:864] += r_1[432:864]

    def ring_copy(slot, src, dst, to):
        return pltpu.make_async_remote_copy(
            src_ref=src, dst_ref=dst, send_sem=r_send.at[slot], recv_sem=r_recv.at[slot],
            device_id=(to, tm, rows), device_id_type=MESH,
        )

    class Stage:
        def __init__(self, slot, src, base, win, hop, cut, pos, plus, minus, m2, p2, bm, bp, out):
            self.src, self.win, self.cut, self.out = src, win, cut, out
            self.bm, self.bp, self.m2, self.p2 = bm, bp, m2, p2

            def at(k, lo, hi):
                return pl.ds(pl.multiple_of(base + ((pos + k) % 4) * hop + lo, 8), hi - lo)

            self.at = at
            self.far_p = ring_copy(slot, src.at[at(2, 0, cut)], m2, plus)
            self.far_m = ring_copy(slot + 1, src.at[at(2, cut, win)], p2, minus)
            self.near_p = ring_copy(slot + 2, src.at[at(1, cut, win)], bm.at[pl.ds(cut, win - cut)], plus)
            self.near_m = ring_copy(slot + 3, src.at[at(3, 0, cut)], bp.at[pl.ds(0, cut)], minus)
            self.sum_p = ring_copy(slot + 4, m2, bm.at[pl.ds(0, cut)], plus)
            self.sum_m = ring_copy(slot + 5, p2, bp.at[pl.ds(cut, win - cut)], minus)
            self.all = (self.far_p, self.far_m, self.near_p, self.near_m, self.sum_p, self.sum_m)

        def start(self):
            for c in self.all[:4]:
                c.start()

        def middle(self):
            self.far_p.wait_recv()
            self.m2[...] += self.src[self.at(1, 0, self.cut), :]
            self.sum_p.start()
            self.far_m.wait_recv()
            self.p2[...] += self.src[self.at(3, self.cut, self.win), :]
            self.sum_m.start()

        def end(self):
            for c in self.all[2:]:
                c.wait_recv()
            self.out[...] = self.src[self.at(0, 0, self.win), :] + self.bm[...] + self.bp[...]

        def drain(self):
            for c in self.all:
                c.wait_send()

    first, second = [], []
    for a in range(2):
        along = ((yy, yp, ym), (zz, zp, zm))
        pos1, plus1, minus1 = along[a]
        pos2, plus2, minus2 = along[1 - a]
        first.append(Stage(
            a * 6, part, a * HALF, WIN1, HOP1, CUT1, pos1, plus1, minus1,
            d2m.at[a], d2p.at[a], bufm.at[a], bufp.at[a], res1.at[a],
        ))
        second.append(Stage(
            12 + a * 6, res1.at[a], 0, WIN2, HOP2, CUT2, pos2, plus2, minus2,
            e2m.at[a], e2p.at[a], cufm.at[a], cufp.at[a], res2.at[a],
        ))
    for st in first:
        st.start()

    w_in.wait()
    pick = (
        lax.broadcasted_iota(jnp.int32, (SL, C), 1)
        == lax.broadcasted_iota(jnp.int32, (SL, C), 0) + j * SL
    ).astype(jnp.bfloat16)
    nt = (((1,), (1,)), ((), ()))
    grads, cots = [], []
    for h in range(2):
        acc = jnp.zeros((144, POS), jnp.float32)
        for hs in range(2):
            dh = h - hs + 1
            for dt in range(3):
                tap = dt * 9 + dh * 3
                w_rows = wv[tap:tap + 3].reshape(144, C)
                c_rows = cot[hs, (2 - dt) * 128:(2 - dt) * 128 + POS, :]
                if hs == h and dt == 2:
                    both = lax.dot_general(
                        jnp.concatenate([w_rows, pick], 0), c_rows, nt, preferred_element_type=jnp.float32
                    )
                    cots.append(both[144:192])
                    acc = acc + both[0:144]
                else:
                    acc = acc + lax.dot_general(w_rows, c_rows, nt, preferred_element_type=jnp.float32)
        grads.append(acc)

    for st in first:
        st.middle()

    t1 = jnp.zeros((SL, 128), jnp.float32)
    t2 = jnp.zeros((SL, 128), jnp.float32)
    for h in range(2):
        for t in range(8):
            sl = slice(t * 128, (t + 1) * 128)
            gl = slice((h * 8 + t) * 128, (h * 8 + t + 1) * 128)
            g0, g1, g2 = (grads[h][k * SL:(k + 1) * SL, sl] for k in range(3))
            g = (
                g1
                + jnp.where(lane == 127, 0.0, pltpu.roll(g0, 127, 1))
                + jnp.where(lane == 0, 0.0, pltpu.roll(g2, 1, 1))
            )
            gn = g * dsil_s[:, gl]
            dsil_s[:, gl] = gn
            t1 = t1 + gn
            t2 = t2 + gn * normed_s[:, gl]
    m1, m2 = group_mean(t1), group_mean(t2)
    rstd_l = stat[...]
    for h in range(2):
        for t in range(8):
            sl = slice(t * 128, (t + 1) * 128)
            gl = slice((h * 8 + t) * 128, (h * 8 + t + 1) * 128)
            out = cots[h][:, sl] + rstd_l * (dsil_s[:, gl] - m1 - normed_s[:, gl] * m2)
            ig_send[:, gl] = out.astype(jnp.bfloat16)

    ig_self = pltpu.make_async_copy(ig_send.at[:, own_lanes], ig_recv.at[mine], loc_sem.at[3])
    ig_self.start()
    igs = []
    for k in range(1, 8):
        p = (j + k) % 8
        lanes = pl.ds(pl.multiple_of((p % 2) * POS + (p // 2) * OWN, OWN), OWN)
        c = pltpu.make_async_remote_copy(
            src_ref=ig_send.at[:, lanes], dst_ref=ig_recv.at[mine],
            send_sem=is_send.at[k - 1], recv_sem=is_recv.at[k - 1],
            device_id=dev(p // 2, p % 2), device_id_type=MESH,
        )
        c.start()
        igs.append(c)

    for st in first:
        st.end()
    for st in second:
        st.start()
    ig_self.wait()
    for c in igs:
        c.wait_recv()
    ig_ref[...] = ig_recv[...].astype(jnp.float32).T.astype(jnp.bfloat16)
    for st in second:
        st.middle()
    for st in second:
        st.end()

    last = jnp.logical_and(yy == 3, zz == 3)
    me = clip * 8 + j

    def scatter(act):
        for a in range(2):
            far, near = ((yy, zz), (zz, yy))[a]

            def body(i, _, a=a, far=far, near=near):
                loc = a * 81 + 20 * far + 5 * near + i
                dh, r = loc // 54, loc % 54
                tap = ((r // 6) // 3) * 9 + dh * 3 + (r // 6) % 3
                tile = tap * 48 + 6 * j + r % 6
                c_to, u = tile // 81, tile % 81
                valid = jnp.logical_or(i < 5, last)
                j1 = jnp.minimum(u // 10, 7)
                twice = jnp.logical_and(valid, jnp.logical_and(u % 10 == 0, jnp.logical_and(u > 0, u < 80)))
                src = res2.at[a, pl.ds(pl.multiple_of(i * 8, 8), 8)]
                act(valid, src, c_to, j1, u - 10 * j1, a * 12 + i)
                act(twice, src, c_to, jnp.maximum(u // 10 - 1, 0), 10, a * 12 + 6 + i)
                return 0

            lax.fori_loop(0, 6, body, 0)

    def fin_copy(src, c_to, j_to, slot, sem):
        return pltpu.make_async_remote_copy(
            src_ref=src, dst_ref=fin.at[pl.ds(pl.multiple_of(slot * 8, 8), 8)],
            send_sem=f_send.at[sem], recv_sem=f_recv.at[0],
            device_id=(c_to, j_to // 2, j_to % 2), device_id_type=MESH,
        )

    def begin(cond, src, c_to, j_to, slot, sem):
        here = c_to * 8 + j_to == me

        @pl.when(jnp.logical_and(cond, here))
        def _():
            pltpu.make_async_copy(
                src, fin.at[pl.ds(pl.multiple_of(slot * 8, 8), 8)], f_recv.at[0]
            ).start()

        @pl.when(jnp.logical_and(cond, jnp.logical_not(here)))
        def _():
            fin_copy(src, c_to, j_to, slot, sem).start()

    def finish(cond, src, c_to, j_to, slot, sem):
        @pl.when(jnp.logical_and(cond, c_to * 8 + j_to != me))
        def _():
            fin_copy(src, c_to, j_to, slot, sem).wait_send()

    scatter(begin)

    for c in sends + xs + igs:
        c.wait_send()
    for st in first + second:
        st.drain()

    pltpu.make_async_copy(fin, fin, f_recv.at[0]).wait()
    for k in range(8):
        @pl.when(j == k)
        def _(k=k):
            wg_ref[...] = fin[k:k + 81, :] * SCALE
    scatter(finish)


def per_device(inputs, cotangent, weight, gain, shift_term):
    f32, bf16 = jnp.float32, jnp.bfloat16
    hbm = pl.BlockSpec(memory_space=pltpu.HBM)
    vmem = pl.BlockSpec(memory_space=pltpu.VMEM)
    dma = pltpu.SemaphoreType.DMA
    ig, wg = pl.pallas_call(
        kernel,
        out_shape=(
            jax.ShapeDtypeStruct((OWN, C), bf16),
            jax.ShapeDtypeStruct((81, C), f32),
        ),
        in_specs=[hbm, hbm, hbm, vmem, vmem],
        out_specs=(vmem, vmem),
        scratch_shapes=[
            pltpu.VMEM((OWN, C), bf16),
            pltpu.VMEM((C, OWN), bf16),
            pltpu.VMEM((SL, 2 * POS), bf16),
            pltpu.VMEM((2, POS + OWN, C), bf16),
            pltpu.VMEM((27, SL, C), bf16),
            pltpu.VMEM((2, C, 128), f32),
            pltpu.VMEM((SL, 128), f32),
            pltpu.VMEM((SL, 2 * POS), f32),
            pltpu.VMEM((SL, 2 * POS), f32),
            pltpu.VMEM((864, POS), bf16),
            pltpu.VMEM((1296, C), f32),
            pltpu.VMEM((SL, 2 * POS), bf16),
            pltpu.VMEM((C, OWN), bf16),
            pltpu.VMEM((2, CUT1, C), f32),
            pltpu.VMEM((2, WIN1 - CUT1, C), f32),
            pltpu.VMEM((2, WIN1, C), f32),
            pltpu.VMEM((2, WIN1, C), f32),
            pltpu.VMEM((2, WIN1, C), f32),
            pltpu.VMEM((2, CUT2, C), f32),
            pltpu.VMEM((2, WIN2 - CUT2, C), f32),
            pltpu.VMEM((2, WIN2, C), f32),
            pltpu.VMEM((2, WIN2, C), f32),
            pltpu.VMEM((2, WIN2, C), f32),
            pltpu.VMEM((88, C), f32),
            dma((4,)), dma((10,)), dma((10,)), dma((7,)), dma((7,)), dma((7,)), dma((7,)),
            dma((24,)), dma((24,)), dma((24,)), dma((1,)),
        ],
        compiler_params=pltpu.CompilerParams(
            collective_id=0, has_side_effects=True, vmem_limit_bytes=56 * 1024 * 1024
        ),
        name="resblock_backward",
    )(
        inputs.reshape(OWN, C),
        cotangent.reshape(OWN, C),
        weight.reshape(27, C, C),
        gain.reshape(1, C),
        shift_term.reshape(1, C),
    )
    return ig.reshape(1, 2, 1, 128, C), wg


def solution(mesh):
    return jax.shard_map(
        per_device,
        mesh=mesh,
        in_specs=(
            P("clip", "tm", "rows", None, None),
            P("clip", "tm", "rows", None, None),
            P(),
            P(),
            P(),
        ),
        out_specs=(P("clip", "tm", "rows", None, None), P(("clip", "tm", "rows"), None)),
        check_vma=False,
    )
```

```python
import jax
import jax.numpy as jnp
from jax import lax
from jax.experimental import pallas as pl
from jax.experimental.pallas import tpu as pltpu
from jax.sharding import PartitionSpec as P

MESH = pl.DeviceIdType.MESH
C = 384
SL = 48
PG = 12
POS = 1024
OWN = 256
EPS = 1e-05
CELLS = 12 * 2048
SCALE = 1.0 / 128
WIN1, HOP1, CUT1 = 168, 160, 88
WIN2, HOP2, CUT2 = 48, 40, 24
HALF = 648


def kernel(
    x_hbm, cot_hbm, w_hbm, gain_ref, shift_ref, ig_ref, fin,
    x_own, x_send, x_all, cot, wv, gb, stat, normed_s, dsil_s, lcat, part,
    ig_send, ig_recv, d2m, d2p, bufm, bufp, res1, e2m, e2p, cufm, cufp, res2,
    loc_sem, cs_send, cs_recv, xs_send, xs_recv, is_send, is_recv, r_send, r_recv, f_send, f_recv,
):
    clip, tm, rows = lax.axis_index("clip"), lax.axis_index("tm"), lax.axis_index("rows")
    x_hi, core = tm // 2, tm % 2
    j = tm * 2 + rows
    yy, zz = clip // 4, clip % 4

    def dev(tm_, rows_):
        return (clip, tm_, rows_)

    def ring(tm_, rows_, step):
        hi, co = tm_ // 2, tm_ % 2
        x = (hi * 2 + rows_ + step + 4) % 4
        return (x // 2) * 2 + co, x % 2

    rt, rr = ring(tm, rows, 1)
    lt, lr = ring(tm, rows, -1)
    ot, orow = ring(tm, rows, 2)
    sib_tm = x_hi * 2 + (1 - core)

    x_in = pltpu.make_async_copy(x_hbm, x_own, loc_sem.at[0])
    x_in.start()
    own_slot = pl.ds(pl.multiple_of(tm * OWN, OWN), OWN)
    c_in = pltpu.make_async_copy(cot_hbm, cot.at[rows, own_slot], loc_sem.at[1])
    c_in.start()
    w_in = pltpu.make_async_copy(
        w_hbm.at[:, pl.ds(pl.multiple_of(j * SL, SL), SL)], wv, loc_sem.at[2]
    )
    w_in.start()

    yp, ym = ((yy + 1) % 4) * 4 + zz, ((yy + 3) % 4) * 4 + zz
    zp, zm = yy * 4 + (zz + 1) % 4, yy * 4 + (zz + 3) % 4
    barrier = pltpu.get_barrier_semaphore()
    for k in range(1, 8):
        p = (j + k) % 8
        pl.semaphore_signal(barrier, inc=1, device_id=dev(p // 2, p % 2), device_id_type=MESH)
    for other in (yp, ym, zp, zm):
        pl.semaphore_signal(barrier, inc=1, device_id=(other, tm, rows), device_id_type=MESH)
    pl.semaphore_wait(barrier, 11)

    def frame(tm_, f):
        return pl.ds(pl.multiple_of(tm_ * OWN + f * 128, 128), 128)

    def cot_copy(slot, src, where, to):
        dst = cot.at[where[0], where[1]]
        return pltpu.make_async_remote_copy(
            src_ref=dst if src is None else src, dst_ref=dst,
            send_sem=cs_send.at[slot], recv_sem=cs_recv.at[slot],
            device_id=dev(*to), device_id_type=MESH,
        )

    right, left, sib = (rt, rr), (lt, lr), (sib_tm, rows)
    sends = []
    for slot, f, to in ((0, 0, right), (2, 1, left), (1, 1, right), (3, 0, left)):
        c = cot_copy(slot, cot_hbm.at[pl.ds(f * 128, 128)], (rows, frame(tm, f)), to)
        c.start()
        sends.append(c)
    c = cot_copy(4, cot_hbm, (rows, own_slot), sib)
    c.start()
    sends.append(c)

    def arrived(slot, where):
        cot_copy(slot, None, where, right).wait_recv()

    cot[0, POS:, :] = jnp.zeros((OWN, C), jnp.bfloat16)
    cot[1, POS:, :] = jnp.zeros((OWN, C), jnp.bfloat16)
    x_in.wait()
    x_send[...] = x_own[...].astype(jnp.float32).T.astype(jnp.bfloat16)
    own_lanes = pl.ds(pl.multiple_of(rows * POS + tm * OWN, OWN), OWN)
    x_self = pltpu.make_async_copy(
        x_send.at[pl.ds(pl.multiple_of(j * SL, SL), SL)], x_all.at[:, own_lanes], loc_sem.at[3]
    )
    x_self.start()
    xs = []
    for k in range(1, 8):
        p = (j + k) % 8
        c = pltpu.make_async_remote_copy(
            src_ref=x_send.at[pl.ds(pl.multiple_of(p * SL, SL), SL)], dst_ref=x_all.at[:, own_lanes],
            send_sem=xs_send.at[k - 1], recv_sem=xs_recv.at[k - 1],
            device_id=dev(p // 2, p % 2), device_id_type=MESH,
        )
        c.start()
        xs.append(c)

    gb[0] = jnp.broadcast_to(gain_ref[...].reshape(1, C), (128, C)).T
    gb[1] = jnp.broadcast_to(shift_ref[...].reshape(1, C), (128, C)).T
    mine = pl.ds(pl.multiple_of(j * SL, SL), SL)
    gain_l, shift_l = gb[0, mine, :], gb[1, mine, :]

    arrived(0, (lr, frame(lt, 0)))
    c = cot_copy(5, None, (lr, frame(lt, 0)), right)
    c.start()
    sends.append(c)
    arrived(2, (rr, frame(rt, 1)))
    c = cot_copy(6, None, (rr, frame(rt, 1)), left)
    c.start()
    sends.append(c)

    x_self.wait()
    for c in xs:
        c.wait_recv()

    row_g = lax.broadcasted_iota(jnp.int32, (SL, SL), 0)
    col_g = lax.broadcasted_iota(jnp.int32, (SL, SL), 1)

    def group_of(i):
        return sum((i >= PG * k).astype(jnp.int32) for k in (1, 2, 3))

    same = (group_of(row_g) == group_of(col_g)).astype(jnp.float32)

    def group_mean(values):
        total = jnp.sum(values, axis=1, keepdims=True)
        return jnp.dot(
            same, jnp.broadcast_to(total, (SL, 128)), precision=lax.Precision.HIGHEST,
            preferred_element_type=jnp.float32,
        ) * (1.0 / CELLS)

    s1 = jnp.zeros((SL, 128), jnp.float32)
    s2 = jnp.zeros((SL, 128), jnp.float32)
    for b in range(16):
        v = x_all[:, b * 128:(b + 1) * 128].astype(jnp.float32)
        s1 = s1 + v
        s2 = s2 + v * v
    mean = group_mean(s1)
    rstd = lax.rsqrt(group_mean(s2) - mean * mean + EPS)
    stat[...] = rstd

    lane = lax.broadcasted_iota(jnp.int32, (SL, 128), 1)
    for h in range(2):
        for dt in range(2):
            for dw in range(3):
                r0 = h * 432 + (dt * 3 + dw) * SL
                lcat[r0:r0 + SL, 0:(2 - dt) * 128] = jnp.zeros((SL, (2 - dt) * 128), jnp.bfloat16)
        for t in range(8):
            b = h * 8 + t
            sl = slice(b * 128, (b + 1) * 128)
            v = x_all[:, sl].astype(jnp.float32)
            normed = (v - mean) * rstd
            pre = normed * gain_l + shift_l
            s = 1.0 / (1.0 + jnp.exp(-pre))
            act = pre * s
            normed_s[:, sl] = normed
            dsil_s[:, sl] = s * (1.0 + pre * (1.0 - s)) * gain_l
            before = jnp.where(lane == 0, 0.0, pltpu.roll(act, 1, 1))
            after = jnp.where(lane == 127, 0.0, pltpu.roll(act, 127, 1))
            for dw, a in ((0, before), (1, act), (2, after)):
                a = a.astype(jnp.bfloat16)
                for dt in range(3):
                    t_out = t + 2 - dt
                    if t_out < 8:
                        r0 = h * 432 + (dt * 3 + dw) * SL
                        lcat[r0:r0 + SL, t_out * 128:(t_out + 1) * 128] = a

    arrived(1, (lr, frame(lt, 1)))
    arrived(3, (rr, frame(rt, 0)))
    for slot, who in ((7, (lt, lr)), (8, (rt, rr))):
        c = cot_copy(slot, None, (who[1], pl.ds(pl.multiple_of(who[0] * OWN, OWN), OWN)), sib)
        c.start()
        sends.append(c)
    arrived(5, (orow, frame(ot, 0)))
    arrived(6, (orow, frame(ot, 1)))
    c = cot_copy(9, None, (orow, pl.ds(pl.multiple_of(ot * OWN, OWN), OWN)), sib)
    c.start()
    sends.append(c)
    c_in.wait()

    def sib_of(who):
        t_ = who[0]
        return pl.ds(pl.multiple_of(((t_ // 2) * 2 + 1 - t_ % 2) * OWN, OWN), OWN)

    arrived(4, (rows, sib_of((tm, rows))))
    arrived(7, (lr, sib_of((lt, lr))))
    arrived(8, (rr, sib_of((rt, rr))))
    arrived(9, (orow, sib_of((ot, orow))))

    r_0 = jnp.dot(lcat[...], cot[0, 0:POS, :], preferred_element_type=jnp.float32)
    part[432:864] = r_0[0:432]
    part[864:1296] = r_0[432:864]
    r_1 = jnp.dot(lcat[...], cot[1, 0:POS, :], preferred_element_type=jnp.float32)
    part[0:432] = r_1[0:432]
    part[432:864] += r_1[432:864]

    def ring_copy(slot, src, dst, to):
        return pltpu.make_async_remote_copy(
            src_ref=src, dst_ref=dst, send_sem=r_send.at[slot], recv_sem=r_recv.at[slot],
            device_id=(to, tm, rows), device_id_type=MESH,
        )

    class Stage:
        def __init__(self, slot, src, base, win, hop, cut, pos, plus, minus, m2, p2, bm, bp, out):
            self.src, self.win, self.cut, self.out = src, win, cut, out
            self.bm, self.bp, self.m2, self.p2 = bm, bp, m2, p2

            def at(k, lo, hi):
                return pl.ds(pl.multiple_of(base + ((pos + k) % 4) * hop + lo, 8), hi - lo)

            self.at = at
            self.far_p = ring_copy(slot, src.at[at(2, 0, cut)], m2, plus)
            self.far_m = ring_copy(slot + 1, src.at[at(2, cut, win)], p2, minus)
            self.near_p = ring_copy(slot + 2, src.at[at(1, cut, win)], bm.at[pl.ds(cut, win - cut)], plus)
            self.near_m = ring_copy(slot + 3, src.at[at(3, 0, cut)], bp.at[pl.ds(0, cut)], minus)
            self.sum_p = ring_copy(slot + 4, m2, bm.at[pl.ds(0, cut)], plus)
            self.sum_m = ring_copy(slot + 5, p2, bp.at[pl.ds(cut, win - cut)], minus)
            self.all = (self.far_p, self.far_m, self.near_p, self.near_m, self.sum_p, self.sum_m)

        def start(self):
            for c in self.all[:4]:
                c.start()

        def middle(self):
            self.far_p.wait_recv()
            self.m2[...] += self.src[self.at(1, 0, self.cut), :]
            self.sum_p.start()
            self.far_m.wait_recv()
            self.p2[...] += self.src[self.at(3, self.cut, self.win), :]
            self.sum_m.start()

        def end(self):
            for c in self.all[2:]:
                c.wait_recv()
            self.out[...] = self.src[self.at(0, 0, self.win), :] + self.bm[...] + self.bp[...]

        def drain(self):
            for c in self.all:
                c.wait_send()

    first, second = [], []
    for a in range(2):
        along = ((yy, yp, ym), (zz, zp, zm))
        pos1, plus1, minus1 = along[a]
        pos2, plus2, minus2 = along[1 - a]
        first.append(Stage(
            a * 6, part, a * HALF, WIN1, HOP1, CUT1, pos1, plus1, minus1,
            d2m.at[a], d2p.at[a], bufm.at[a], bufp.at[a], res1.at[a],
        ))
        second.append(Stage(
            12 + a * 6, res1.at[a], 0, WIN2, HOP2, CUT2, pos2, plus2, minus2,
            e2m.at[a], e2p.at[a], cufm.at[a], cufp.at[a], res2.at[a],
        ))
    for st in first:
        st.start()

    w_in.wait()
    pick = (
        lax.broadcasted_iota(jnp.int32, (SL, C), 1)
        == lax.broadcasted_iota(jnp.int32, (SL, C), 0) + j * SL
    ).astype(jnp.bfloat16)
    nt = (((1,), (1,)), ((), ()))
    grads, cots = [], []
    for h in range(2):
        acc = jnp.zeros((144, POS), jnp.float32)
        for hs in range(2):
            dh = h - hs + 1
            for dt in range(3):
                tap = dt * 9 + dh * 3
                w_rows = wv[tap:tap + 3].reshape(144, C)
                c_rows = cot[hs, (2 - dt) * 128:(2 - dt) * 128 + POS, :]
                if hs == h and dt == 2:
                    both = lax.dot_general(
                        jnp.concatenate([w_rows, pick], 0), c_rows, nt, preferred_element_type=jnp.float32
                    )
                    cots.append(both[144:192])
                    acc = acc + both[0:144]
                else:
                    acc = acc + lax.dot_general(w_rows, c_rows, nt, preferred_element_type=jnp.float32)
        grads.append(acc)

    for st in first:
        st.middle()

    t1 = jnp.zeros((SL, 128), jnp.float32)
    t2 = jnp.zeros((SL, 128), jnp.float32)
    for h in range(2):
        for t in range(8):
            sl = slice(t * 128, (t + 1) * 128)
            gl = slice((h * 8 + t) * 128, (h * 8 + t + 1) * 128)
            g0, g1, g2 = (grads[h][k * SL:(k + 1) * SL, sl] for k in range(3))
            g = (
                g1
                + jnp.where(lane == 127, 0.0, pltpu.roll(g0, 127, 1))
                + jnp.where(lane == 0, 0.0, pltpu.roll(g2, 1, 1))
            )
            gn = g * dsil_s[:, gl]
            dsil_s[:, gl] = gn
            t1 = t1 + gn
            t2 = t2 + gn * normed_s[:, gl]
    m1, m2 = group_mean(t1), group_mean(t2)
    rstd_l = stat[...]
    for h in range(2):
        for t in range(8):
            sl = slice(t * 128, (t + 1) * 128)
            gl = slice((h * 8 + t) * 128, (h * 8 + t + 1) * 128)
            out = cots[h][:, sl] + rstd_l * (dsil_s[:, gl] - m1 - normed_s[:, gl] * m2)
            ig_send[:, gl] = out.astype(jnp.bfloat16)

    ig_self = pltpu.make_async_copy(ig_send.at[:, own_lanes], ig_recv.at[mine], loc_sem.at[3])
    ig_self.start()
    igs = []
    for k in range(1, 8):
        p = (j + k) % 8
        lanes = pl.ds(pl.multiple_of((p % 2) * POS + (p // 2) * OWN, OWN), OWN)
        c = pltpu.make_async_remote_copy(
            src_ref=ig_send.at[:, lanes], dst_ref=ig_recv.at[mine],
            send_sem=is_send.at[k - 1], recv_sem=is_recv.at[k - 1],
            device_id=dev(p // 2, p % 2), device_id_type=MESH,
        )
        c.start()
        igs.append(c)

    for st in first:
        st.end()
    for st in second:
        st.start()
    ig_self.wait()
    for c in igs:
        c.wait_recv()
    ig_ref[...] = ig_recv[...].astype(jnp.float32).T.astype(jnp.bfloat16)
    for st in second:
        st.middle()
    for st in second:
        st.end()

    last = jnp.logical_and(yy == 3, zz == 3)
    me = clip * 8 + j

    def scatter(act):
        for a in range(2):
            far, near = ((yy, zz), (zz, yy))[a]

            def body(i, _, a=a, far=far, near=near):
                loc = a * 81 + 20 * far + 5 * near + i
                dh, r = loc // 54, loc % 54
                tap = ((r // 6) // 3) * 9 + dh * 3 + (r // 6) % 3
                tile = tap * 48 + 6 * j + r % 6
                c_to, u = tile // 81, tile % 81
                valid = jnp.logical_or(i < 5, last)
                j1 = jnp.minimum(u // 10, 7)
                twice = jnp.logical_and(valid, jnp.logical_and(u % 10 == 0, jnp.logical_and(u > 0, u < 80)))
                src = res2.at[a, pl.ds(pl.multiple_of(i * 8, 8), 8)]
                act(valid, src, c_to, j1, u - 10 * j1, a * 12 + i)
                act(twice, src, c_to, jnp.maximum(u // 10 - 1, 0), 10, a * 12 + 6 + i)
                return 0

            lax.fori_loop(0, 6, body, 0)

    def fin_copy(src, c_to, j_to, slot, sem):
        return pltpu.make_async_remote_copy(
            src_ref=src, dst_ref=fin.at[pl.ds(pl.multiple_of(slot * 8, 8), 8)],
            send_sem=f_send.at[sem], recv_sem=f_recv.at[0],
            device_id=(c_to, j_to // 2, j_to % 2), device_id_type=MESH,
        )

    def begin(cond, src, c_to, j_to, slot, sem):
        here = c_to * 8 + j_to == me

        @pl.when(jnp.logical_and(cond, here))
        def _():
            pltpu.make_async_copy(
                src, fin.at[pl.ds(pl.multiple_of(slot * 8, 8), 8)], f_recv.at[0]
            ).start()

        @pl.when(jnp.logical_and(cond, jnp.logical_not(here)))
        def _():
            fin_copy(src, c_to, j_to, slot, sem).start()

    def finish(cond, src, c_to, j_to, slot, sem):
        @pl.when(jnp.logical_and(cond, c_to * 8 + j_to != me))
        def _():
            fin_copy(src, c_to, j_to, slot, sem).wait_send()

    scatter(begin)

    for c in sends + xs + igs:
        c.wait_send()
    for st in first + second:
        st.drain()

    pltpu.make_async_copy(fin, fin, f_recv.at[0]).wait()
    scatter(finish)


def write_out(ig_in, fin, ig_out, wg_out, sem):
    copy = pltpu.make_async_copy(ig_in, ig_out, sem)
    copy.start()
    j = lax.axis_index("tm") * 2 + lax.axis_index("rows")
    for k in range(8):
        @pl.when(j == k)
        def _(k=k):
            wg_out[...] = fin[k:k + 81, :] * SCALE
    copy.wait()


def per_device(inputs, cotangent, weight, gain, shift_term):
    f32, bf16 = jnp.float32, jnp.bfloat16
    hbm = pl.BlockSpec(memory_space=pltpu.HBM)
    vmem = pl.BlockSpec(memory_space=pltpu.VMEM)
    dma = pltpu.SemaphoreType.DMA
    ig, fin = pl.pallas_call(
        kernel,
        out_shape=(pltpu.VMEM((OWN, C), bf16), pltpu.VMEM((88, C), f32)),
        in_specs=[hbm, hbm, hbm, vmem, vmem],
        out_specs=(vmem, vmem),
        scratch_shapes=[
            pltpu.VMEM((OWN, C), bf16),
            pltpu.VMEM((C, OWN), bf16),
            pltpu.VMEM((SL, 2 * POS), bf16),
            pltpu.VMEM((2, POS + OWN, C), bf16),
            pltpu.VMEM((27, SL, C), bf16),
            pltpu.VMEM((2, C, 128), f32),
            pltpu.VMEM((SL, 128), f32),
            pltpu.VMEM((SL, 2 * POS), f32),
            pltpu.VMEM((SL, 2 * POS), f32),
            pltpu.VMEM((864, POS), bf16),
            pltpu.VMEM((1296, C), f32),
            pltpu.VMEM((SL, 2 * POS), bf16),
            pltpu.VMEM((C, OWN), bf16),
            pltpu.VMEM((2, CUT1, C), f32),
            pltpu.VMEM((2, WIN1 - CUT1, C), f32),
            pltpu.VMEM((2, WIN1, C), f32),
            pltpu.VMEM((2, WIN1, C), f32),
            pltpu.VMEM((2, WIN1, C), f32),
            pltpu.VMEM((2, CUT2, C), f32),
            pltpu.VMEM((2, WIN2 - CUT2, C), f32),
            pltpu.VMEM((2, WIN2, C), f32),
            pltpu.VMEM((2, WIN2, C), f32),
            pltpu.VMEM((2, WIN2, C), f32),
            dma((4,)), dma((10,)), dma((10,)), dma((7,)), dma((7,)), dma((7,)), dma((7,)),
            dma((24,)), dma((24,)), dma((24,)), dma((1,)),
        ],
        compiler_params=pltpu.CompilerParams(
            collective_id=0, has_side_effects=True, vmem_limit_bytes=56 * 1024 * 1024
        ),
        name="resblock_backward",
    )(
        inputs.reshape(OWN, C),
        cotangent.reshape(OWN, C),
        weight.reshape(27, C, C),
        gain,
        shift_term,
    )
    ig, fin = (pltpu.with_memory_space_constraint(v, pltpu.VMEM) for v in (ig, fin))
    ig, wg = pl.pallas_call(
        write_out,
        out_shape=(
            jax.ShapeDtypeStruct((OWN, C), bf16),
            jax.ShapeDtypeStruct((81, C), f32),
        ),
        in_specs=[vmem, vmem],
        out_specs=(hbm, vmem),
        scratch_shapes=[dma],
        name="write_out",
    )(ig, fin)
    return ig.reshape(1, 2, 1, 128, C), wg


def solution(mesh):
    return jax.shard_map(
        per_device,
        mesh=mesh,
        in_specs=(
            P("clip", "tm", "rows", None, None),
            P("clip", "tm", "rows", None, None),
            P(),
            P(),
            P(),
        ),
        out_specs=(P("clip", "tm", "rows", None, None), P(("clip", "tm", "rows"), None)),
        check_vma=False,
    )
```

```python
import jax
import jax.numpy as jnp
from jax import lax
from jax.experimental import pallas as pl
from jax.experimental.pallas import tpu as pltpu
from jax.sharding import PartitionSpec as P

MESH = pl.DeviceIdType.MESH
C = 384
SL = 48
PG = 12
POS = 1024
OWN = 256
EPS = 1e-05
CELLS = 12 * 2048
SCALE = 1.0 / 128
ODD = (1, 7, 13, 21, 9, 15, 23, 3, 11, 17, 5, 19, 25)
ORDER = tuple(range(0, 27, 2)) + ODD
WIN1, CUT1 = 168, 88
BASES, HOPS = (0, 672), (168, 152)
WIN2, HOP2 = 48, 40
GCH = ((0, 384),)
NG = len(GCH)
CH = ((0, 384),)
NCH = len(CH)


MSG = 96
SPAN = 125.0


def encode(values):
    n, w = values.shape
    tiles = values.reshape(n // 8, 8, w)
    top = jnp.max(jnp.abs(tiles), axis=0) * 1.01 + 1e-30
    top = top.astype(jnp.bfloat16).astype(jnp.float32)
    code = jnp.exp2(tiles * (SPAN / top)[None]).reshape(n, w)
    return jnp.concatenate([code] + [top] * ((MSG - n) // 8), 0).astype(jnp.bfloat16)


def decode(message, n):
    wide = message.astype(jnp.float32)
    top = wide[n:n + 8] * (1.0 / SPAN)
    w = wide.shape[1]
    return (jnp.log2(wide[0:n]).reshape(n // 8, 8, w) * top[None]).reshape(n, w)


def kernel(
    x_hbm, cot_hbm, w_hbm, gain_ref, shift_ref, ig_ref, fin,
    x_own, x_send, x_all, cot, wv, gb, stat, normed_s, dsil_s, lcat, part,
    ig_send, ig_recv, out_b, in_b, res1, ebuf, res2,
    loc_sem, cs_send, cs_recv, xs_send, xs_recv, is_send, is_recv, r_send, r_recv, f_send, f_recv,
):
    clip, tm, rows = lax.axis_index("clip"), lax.axis_index("tm"), lax.axis_index("rows")
    x_hi, core = tm // 2, tm % 2
    j = tm * 2 + rows
    yy, zz = clip // 4, clip % 4

    def dev(tm_, rows_):
        return (clip, tm_, rows_)

    def ring(tm_, rows_, step):
        hi, co = tm_ // 2, tm_ % 2
        x = (hi * 2 + rows_ + step + 4) % 4
        return (x // 2) * 2 + co, x % 2

    rt, rr = ring(tm, rows, 1)
    lt, lr = ring(tm, rows, -1)
    ot, orow = ring(tm, rows, 2)
    sib_tm = x_hi * 2 + (1 - core)

    x_in = pltpu.make_async_copy(x_hbm, x_own, loc_sem.at[0])
    x_in.start()
    own_slot = pl.ds(pl.multiple_of(tm * OWN, OWN), OWN)
    c_in = []
    for c in range(NG):
        copy = pltpu.make_async_copy(
            cot_hbm.at[:, pl.ds(*GCH[c])], cot.at[rows, own_slot, pl.ds(*GCH[c])], loc_sem.at[4 + c]
        )
        copy.start()
        c_in.append(copy)
    w_in = pltpu.make_async_copy(
        w_hbm.at[:, pl.ds(pl.multiple_of(j * SL, SL), SL)], wv, loc_sem.at[2]
    )
    w_in.start()

    yp, ym = ((yy + 1) % 4) * 4 + zz, ((yy + 3) % 4) * 4 + zz
    yo, zo = ((yy + 2) % 4) * 4 + zz, yy * 4 + (zz + 2) % 4
    zp, zm = yy * 4 + (zz + 1) % 4, yy * 4 + (zz + 3) % 4
    barrier = pltpu.get_barrier_semaphore()
    for k in range(1, 8):
        p = (j + k) % 8
        pl.semaphore_signal(barrier, inc=1, device_id=dev(p // 2, p % 2), device_id_type=MESH)
    for other in (yp, ym, zp, zm):
        pl.semaphore_signal(barrier, inc=1, device_id=(other, tm, rows), device_id_type=MESH)

    x_in.wait()
    x_send[...] = x_own[...].astype(jnp.float32).T.astype(jnp.bfloat16)
    gb[0] = jnp.broadcast_to(gain_ref[...].reshape(1, C), (128, C)).T
    gb[1] = jnp.broadcast_to(shift_ref[...].reshape(1, C), (128, C)).T
    for h in range(2):
        cot[h, POS:, :] = jnp.zeros((OWN, C), jnp.bfloat16)
    pl.semaphore_wait(barrier, 11)

    def frame(tm_, f):
        return pl.ds(pl.multiple_of(tm_ * OWN + f * 128, 128), 128)

    def cot_copy(ch, slot, where, to):
        ref = cot.at[where[0], where[1], pl.ds(*GCH[ch])]
        return pltpu.make_async_remote_copy(
            src_ref=ref, dst_ref=ref,
            send_sem=cs_send.at[ch, slot], recv_sem=cs_recv.at[ch, slot],
            device_id=dev(*to), device_id_type=MESH,
        )

    right, left, sib = (rt, rr), (lt, lr), (sib_tm, rows)
    sends = []

    def send(ch, slot, where, to):
        copy = cot_copy(ch, slot, where, to)
        copy.start()
        sends.append(copy)

    def arrived(ch, slot, where):
        cot_copy(ch, slot, where, right).wait_recv()

    def whole(who):
        return who[1], pl.ds(pl.multiple_of(who[0] * OWN, OWN), OWN)

    def sib_of(who):
        return whole((who[0] + 1 - 2 * (who[0] % 2), who[1]))

    def own(ch):
        c_in[ch].wait()
        send(ch, 0, (rows, frame(tm, 0)), right)
        send(ch, 2, (rows, frame(tm, 1)), left)
        send(ch, 1, (rows, frame(tm, 1)), right)
        send(ch, 3, (rows, frame(tm, 0)), left)
        send(ch, 4, (rows, own_slot), sib)

    def fwd1(ch):
        arrived(ch, 0, (lr, frame(lt, 0)))
        send(ch, 5, (lr, frame(lt, 0)), right)
        arrived(ch, 2, (rr, frame(rt, 1)))
        send(ch, 6, (rr, frame(rt, 1)), left)

    def fwd2(ch):
        arrived(ch, 1, (lr, frame(lt, 1)))
        send(ch, 7, whole((lt, lr)), sib)
        arrived(ch, 3, (rr, frame(rt, 0)))
        send(ch, 8, whole((rt, rr)), sib)

    def fwd3(ch):
        arrived(ch, 5, (orow, frame(ot, 0)))
        arrived(ch, 6, (orow, frame(ot, 1)))
        send(ch, 9, whole((ot, orow)), sib)

    def gathered(ch):
        arrived(ch, 4, sib_of((tm, rows)))
        arrived(ch, 7, sib_of((lt, lr)))
        arrived(ch, 8, sib_of((rt, rr)))
        arrived(ch, 9, sib_of((ot, orow)))

    own(0)

    own_lanes = pl.ds(pl.multiple_of(rows * POS + tm * OWN, OWN), OWN)
    x_self = pltpu.make_async_copy(
        x_send.at[pl.ds(pl.multiple_of(j * SL, SL), SL)], x_all.at[:, own_lanes], loc_sem.at[3]
    )
    x_self.start()
    xs = []
    for k in range(1, 8):
        p = (j + k) % 8
        c = pltpu.make_async_remote_copy(
            src_ref=x_send.at[pl.ds(pl.multiple_of(p * SL, SL), SL)], dst_ref=x_all.at[:, own_lanes],
            send_sem=xs_send.at[k - 1], recv_sem=xs_recv.at[k - 1],
            device_id=dev(p // 2, p % 2), device_id_type=MESH,
        )
        c.start()
        xs.append(c)

    mine = pl.ds(pl.multiple_of(j * SL, SL), SL)
    gain_l, shift_l = gb[0, mine, :], gb[1, mine, :]

    fwd1(0)

    me = clip * 8 + j
    jobs = []
    for a in range(2):
        far, near = ((yy, zz), (zz, yy))[a]
        again = []
        for i in range(6):
            loc = (21, 19)[a] * far + 5 * near + i
            n = loc // 6
            tap = 2 * n if a == 0 else sum(jnp.where(n == k, t, 0) for k, t in enumerate(ODD))
            r = loc % 6
            tile = tap * 48 + 6 * j + r
            c_to, u = tile // 81, tile % 81
            j_to = jnp.minimum(u // 10, 7)
            if i < 4:
                ok = jnp.bool_(True)
            elif a == 0:
                ok = jnp.logical_or(i < 5, near == 3)
            elif i == 4:
                ok = jnp.logical_or(near < 3, far == 3)
            else:
                ok = jnp.logical_and(near == 3, far == 3)
            jobs.append((ok, c_to * 8 + j_to, u - 10 * j_to))
            edge = jnp.logical_and(u - 10 * j_to == 0, j_to > 0)
            again.append((jnp.logical_and(ok, edge), c_to * 8 + jnp.maximum(j_to - 1, 0), 10))
        jobs += again

    x_self.wait()
    for c in xs:
        c.wait_recv()

    row_g = lax.broadcasted_iota(jnp.int32, (SL, SL), 0)
    col_g = lax.broadcasted_iota(jnp.int32, (SL, SL), 1)

    def group_of(i):
        return sum((i >= PG * k).astype(jnp.int32) for k in (1, 2, 3))

    same = (group_of(row_g) == group_of(col_g)).astype(jnp.float32)

    def group_mean(values):
        total = jnp.sum(values, axis=1, keepdims=True)
        return jnp.dot(
            same, jnp.broadcast_to(total, (SL, 128)), precision=lax.Precision.HIGHEST,
            preferred_element_type=jnp.float32,
        ) * (1.0 / CELLS)

    s1 = jnp.zeros((SL, 128), jnp.float32)
    s2 = jnp.zeros((SL, 128), jnp.float32)
    for b in range(16):
        v = x_all[:, b * 128:(b + 1) * 128].astype(jnp.float32)
        s1 = s1 + v
        s2 = s2 + v * v
    mean = group_mean(s1)
    rstd = lax.rsqrt(group_mean(s2) - mean * mean + EPS)
    stat[...] = rstd

    lane = lax.broadcasted_iota(jnp.int32, (SL, 128), 1)
    for h in range(2):
        for dt in range(2):
            for dw in range(3):
                r0 = h * 432 + (dt * 3 + dw) * SL
                lcat[r0:r0 + SL, 0:(2 - dt) * 128] = jnp.zeros((SL, (2 - dt) * 128), jnp.bfloat16)
        for t in range(8):
            b = h * 8 + t
            sl = slice(b * 128, (b + 1) * 128)
            v = x_all[:, sl].astype(jnp.float32)
            normed = (v - mean) * rstd
            pre = normed * gain_l + shift_l
            s = 1.0 / (1.0 + jnp.exp(-pre))
            act = pre * s
            normed_s[:, sl] = normed
            dsil_s[:, sl] = s * (1.0 + pre * (1.0 - s)) * gain_l
            before = jnp.where(lane == 0, 0.0, pltpu.roll(act, 1, 1))
            after = jnp.where(lane == 127, 0.0, pltpu.roll(act, 127, 1))
            for dw, a in ((0, before), (1, act), (2, after)):
                a = a.astype(jnp.bfloat16)
                for dt in range(3):
                    t_out = t + 2 - dt
                    if t_out < 8:
                        r0 = h * 432 + (dt * 3 + dw) * SL
                        lcat[r0:r0 + SL, t_out * 128:(t_out + 1) * 128] = a

    def weight_grad(ch):
        lo, hi = CH[ch][0], sum(CH[ch])
        r_0 = jnp.dot(lcat[...], cot[0, 0:POS, lo:hi], preferred_element_type=jnp.float32)
        r_1 = jnp.dot(lcat[...], cot[1, 0:POS, lo:hi], preferred_element_type=jnp.float32)
        for dt in range(3):
            for dw in range(3):
                q = (dt * 3 + dw) * SL
                near = [r[k:k + SL] for r in (r_0, r_1) for k in (q, q + 432)]
                for dh, v in ((0, near[2]), (1, near[0] + near[3]), (2, near[1])):
                    r0 = ORDER.index(dt * 9 + dh * 3 + dw) * SL
                    part[r0:r0 + SL, lo:hi] = v

    def ring_copy(ch, slot, src, dst, to):
        return pltpu.make_async_remote_copy(
            src_ref=src, dst_ref=dst, send_sem=r_send.at[ch, slot], recv_sem=r_recv.at[ch, slot],
            device_id=(to, tm, rows), device_id_type=MESH,
        )

    class Ring:
        def __init__(self, ch, slot, src, base, hop, pos, plus, minus, out_b, in_b, out):
            self.src, self.out, self.out_b, self.in_b = src, out, out_b, in_b

            def at(k, lo, hi):
                return pl.ds(pl.multiple_of(base + ((pos + k) % 4) * hop + lo, 8), hi - lo)

            self.at = at
            self.all = [
                ring_copy(ch, slot + k, out_b.at[k], in_b.at[k], minus if k % 2 else plus) for k in range(6)
            ]

        def put(self, k, values):
            self.out_b[k] = encode(values)
            self.all[k].start()

        def got(self, k, n):
            self.all[k].wait_recv()
            return decode(self.in_b[k], n)

        def start(self):
            self.put(0, self.src[self.at(2, 0, CUT1), :])
            self.put(1, self.src[self.at(2, CUT1, WIN1), :])

        def near(self):
            self.put(2, self.src[self.at(1, CUT1, WIN1), :])
            self.put(3, self.src[self.at(3, 0, CUT1), :])

        def middle(self):
            self.put(4, self.got(0, CUT1) + self.src[self.at(1, 0, CUT1), :])
            self.put(5, self.got(1, WIN1 - CUT1) + self.src[self.at(3, CUT1, WIN1), :])

        def end(self):
            self.out[0:CUT1] = self.src[self.at(0, 0, CUT1), :] + self.got(3, CUT1) + self.got(4, CUT1)
            self.out[CUT1:WIN1] = (
                self.src[self.at(0, CUT1, WIN1), :] + self.got(2, WIN1 - CUT1) + self.got(5, WIN1 - CUT1)
            )

    class Direct:
        def __init__(self, ch, slot, src, pos, to, bufs, out):
            self.src, self.bufs, self.out = src, bufs, out
            self.at = [pl.ds(pl.multiple_of(((pos + k) % 4) * HOP2, 8), WIN2) for k in range(4)]
            self.all = [
                ring_copy(ch, slot + k - 1, src.at[self.at[k]], bufs.at[k - 1], to[k - 1]) for k in (2, 1, 3)
            ]

        def start(self):
            for c in self.all:
                c.start()

        def end(self):
            for c in self.all:
                c.wait_recv()
            self.out[...] = self.src[self.at[0], :] + self.bufs[0] + self.bufs[1] + self.bufs[2]

    first, second = [], []
    for c in range(NCH):
        for a in range(2):
            lanes = pl.ds(*CH[c])
            along = ((yy, yp, ym, yo), (zz, zp, zm, zo))
            pos1, plus1, minus1, _ = along[a]
            pos2, plus2, minus2, far2 = along[1 - a]
            first.append(Ring(
                c, a * 6, part.at[:, lanes], BASES[a], HOPS[a], pos1, plus1, minus1,
                out_b.at[a, :, :, lanes], in_b.at[a, :, :, lanes], res1.at[a, :, lanes],
            ))
            second.append(Direct(
                c, 12 + a * 3, res1.at[a, :, lanes], pos2, (plus2, far2, minus2),
                ebuf.at[a, :, :, lanes], res2.at[a, :, lanes],
            ))

    def start1(ch):
        for st in first[2 * ch:2 * ch + 2]:
            st.start()

    def near1(ch):
        for st in first[2 * ch:2 * ch + 2]:
            st.near()

    def mid1(ch):
        for st in first[2 * ch:2 * ch + 2]:
            st.middle()

    def turn(ch):
        for st, nxt in zip(first[2 * ch:2 * ch + 2], second[2 * ch:2 * ch + 2]):
            st.end()
            nxt.start()

    def end2(ch):
        for st in second[2 * ch:2 * ch + 2]:
            st.end()
        scatter(ch, begin)

    nt = (((1,), (1,)), ((), ()))
    grads, cots = [], []

    def grad_active(h):
        acc = jnp.zeros((144, POS), jnp.float32)
        for hs in range(2):
            dh = h - hs + 1
            for dt in range(3):
                tap = dt * 9 + dh * 3
                w_rows = wv[tap:tap + 3].reshape(144, C)
                c_rows = cot[hs, (2 - dt) * 128:(2 - dt) * 128 + POS, :]
                if hs == h and dt == 2:
                    both = lax.dot_general(
                        jnp.concatenate([w_rows, pick], 0), c_rows, nt, preferred_element_type=jnp.float32
                    )
                    cots.append(both[144:192])
                    acc = acc + both[0:144]
                else:
                    acc = acc + lax.dot_general(w_rows, c_rows, nt, preferred_element_type=jnp.float32)
        grads.append(acc)

    def input_grad():
        t1 = jnp.zeros((SL, 128), jnp.float32)
        t2 = jnp.zeros((SL, 128), jnp.float32)
        for h in range(2):
            for t in range(8):
                sl = slice(t * 128, (t + 1) * 128)
                gl = slice((h * 8 + t) * 128, (h * 8 + t + 1) * 128)
                g0, g1, g2 = (grads[h][k * SL:(k + 1) * SL, sl] for k in range(3))
                g = (
                    g1
                    + jnp.where(lane == 127, 0.0, pltpu.roll(g0, 127, 1))
                    + jnp.where(lane == 0, 0.0, pltpu.roll(g2, 1, 1))
                )
                gn = g * dsil_s[:, gl]
                dsil_s[:, gl] = gn
                t1 = t1 + gn
                t2 = t2 + gn * normed_s[:, gl]
        m1, m2 = group_mean(t1), group_mean(t2)
        rstd_l = stat[...]
        for h in range(2):
            for t in range(8):
                sl = slice(t * 128, (t + 1) * 128)
                gl = slice((h * 8 + t) * 128, (h * 8 + t + 1) * 128)
                out = cots[h][:, sl] + rstd_l * (dsil_s[:, gl] - m1 - normed_s[:, gl] * m2)
                ig_send[:, gl] = out.astype(jnp.bfloat16)

    ig_self = pltpu.make_async_copy(ig_send.at[:, own_lanes], ig_recv.at[mine], loc_sem.at[3])
    igs = []
    for k in range(1, 8):
        p = (j + k) % 8
        lanes = pl.ds(pl.multiple_of((p % 2) * POS + (p // 2) * OWN, OWN), OWN)
        igs.append(pltpu.make_async_remote_copy(
            src_ref=ig_send.at[:, lanes], dst_ref=ig_recv.at[mine],
            send_sem=is_send.at[k - 1], recv_sem=is_recv.at[k - 1],
            device_id=dev(p // 2, p % 2), device_id_type=MESH,
        ))

    def ig_out():
        ig_self.wait()
        for c in igs:
            c.wait_recv()
        ig_ref[...] = ig_recv[...].astype(jnp.float32).T.astype(jnp.bfloat16)

    def scatter(ch, act):
        for n, (ok, d_to, slot) in enumerate(jobs):
            src = res2.at[n // 12, pl.ds(n % 6 * 8, 8), pl.ds(*CH[ch])]
            act(ch, n, ok, src, d_to, slot)

    def fin_at(ch, slot):
        return fin.at[pl.ds(pl.multiple_of(slot * 8, 8), 8), pl.ds(*CH[ch])]

    def fin_copy(ch, n, src, d_to, slot):
        return pltpu.make_async_remote_copy(
            src_ref=src, dst_ref=fin_at(ch, slot), send_sem=f_send.at[ch, n], recv_sem=f_recv.at[ch],
            device_id=(d_to // 8, d_to % 8 // 2, d_to % 2), device_id_type=MESH,
        )

    def begin(ch, n, ok, src, d_to, slot):
        @pl.when(jnp.logical_and(ok, d_to == me))
        def _():
            pltpu.make_async_copy(src, fin_at(ch, slot), f_recv.at[ch]).start()

        @pl.when(jnp.logical_and(ok, d_to != me))
        def _():
            fin_copy(ch, n, src, d_to, slot).start()

    def finish(ch, n, ok, src, d_to, slot):
        @pl.when(jnp.logical_and(ok, d_to != me))
        def _():
            fin_copy(ch, n, src, d_to, slot).wait_send()

    fwd2(0)
    fwd3(0)
    gathered(0)
    weight_grad(0)
    start1(0)
    near1(0)
    w_in.wait()
    pick = (
        lax.broadcasted_iota(jnp.int32, (SL, C), 1)
        == lax.broadcasted_iota(jnp.int32, (SL, C), 0) + j * SL
    ).astype(jnp.bfloat16)
    grad_active(0)
    grad_active(1)
    mid1(0)
    input_grad()
    for c in [ig_self] + igs:
        c.start()
    turn(0)
    ig_out()
    end2(0)

    for c in sends + xs + igs:
        c.wait_send()
    for st in first + second:
        for c in st.all:
            c.wait_send()
    for c in range(NCH):
        lanes = fin.at[:, pl.ds(*CH[c])]
        pltpu.make_async_copy(lanes, lanes, f_recv.at[c]).wait()
    for c in range(NCH):
        scatter(c, finish)


def write_out(ig_in, fin, ig_out, wg_out, sem):
    copy = pltpu.make_async_copy(ig_in, ig_out, sem)
    copy.start()
    j = lax.axis_index("tm") * 2 + lax.axis_index("rows")
    for k in range(8):
        @pl.when(j == k)
        def _(k=k):
            wg_out[...] = fin[k:k + 81, :] * SCALE
    copy.wait()


def per_device(inputs, cotangent, weight, gain, shift_term):
    f32, bf16 = jnp.float32, jnp.bfloat16
    hbm = pl.BlockSpec(memory_space=pltpu.HBM)
    vmem = pl.BlockSpec(memory_space=pltpu.VMEM)
    dma = pltpu.SemaphoreType.DMA
    ig, fin = pl.pallas_call(
        kernel,
        out_shape=(pltpu.VMEM((OWN, C), bf16), pltpu.VMEM((88, C), f32)),
        in_specs=[hbm, hbm, hbm, vmem, vmem],
        out_specs=(vmem, vmem),
        scratch_shapes=[
            pltpu.VMEM((OWN, C), bf16),
            pltpu.VMEM((C, OWN), bf16),
            pltpu.VMEM((SL, 2 * POS), bf16),
            pltpu.VMEM((2, POS + OWN, C), bf16),
            pltpu.VMEM((27, SL, C), bf16),
            pltpu.VMEM((2, C, 128), f32),
            pltpu.VMEM((SL, 128), f32),
            pltpu.VMEM((SL, 2 * POS), f32),
            pltpu.VMEM((SL, 2 * POS), f32),
            pltpu.VMEM((864, POS), bf16),
            pltpu.VMEM((1296, C), f32),
            pltpu.VMEM((SL, 2 * POS), bf16),
            pltpu.VMEM((C, OWN), bf16),
            pltpu.VMEM((2, 6, MSG, C), bf16),
            pltpu.VMEM((2, 6, MSG, C), bf16),
            pltpu.VMEM((2, WIN1, C), f32),
            pltpu.VMEM((2, 3, WIN2, C), f32),
            pltpu.VMEM((2, WIN2, C), f32),
            dma((4 + NG,)), dma((NG, 10)), dma((NG, 10)), dma((7,)), dma((7,)), dma((7,)), dma((7,)),
            dma((NCH, 18)), dma((NCH, 18)), dma((NCH, 24)), dma((NCH,)),
        ],
        compiler_params=pltpu.CompilerParams(
            collective_id=0, has_side_effects=True, vmem_limit_bytes=56 * 1024 * 1024
        ),
        name="resblock_backward",
    )(
        inputs.reshape(OWN, C),
        cotangent.reshape(OWN, C),
        weight.reshape(27, C, C),
        gain,
        shift_term,
    )
    ig, fin = (pltpu.with_memory_space_constraint(v, pltpu.VMEM) for v in (ig, fin))
    ig, wg = pl.pallas_call(
        write_out,
        out_shape=(
            jax.ShapeDtypeStruct((OWN, C), bf16),
            jax.ShapeDtypeStruct((81, C), f32),
        ),
        in_specs=[vmem, vmem],
        out_specs=(hbm, vmem),
        scratch_shapes=[dma],
        name="write_out",
    )(ig, fin)
    return ig.reshape(1, 2, 1, 128, C), wg


def solution(mesh):
    return jax.shard_map(
        per_device,
        mesh=mesh,
        in_specs=(
            P("clip", "tm", "rows", None, None),
            P("clip", "tm", "rows", None, None),
            P(),
            P(),
            P(),
        ),
        out_specs=(P("clip", "tm", "rows", None, None), P(("clip", "tm", "rows"), None)),
        check_vma=False,
    )
```

```python
import jax
import jax.numpy as jnp
from jax import lax
from jax.experimental import pallas as pl
from jax.experimental.pallas import tpu as pltpu
from jax.sharding import PartitionSpec as P

MESH = pl.DeviceIdType.MESH
C = 384
SL = 48
PG = 12
POS = 1024
OWN = 256
EPS = 1e-05
CELLS = 12 * 2048
SCALE = 1.0 / 128
ODD = (1, 7, 13, 21, 9, 15, 23, 3, 11, 17, 5, 19, 25)
ORDER = tuple(range(0, 27, 2)) + ODD
WIN1, CUT1 = 168, 88
BASES, HOPS = (0, 672), (168, 152)
WIN2, HOP2 = 48, 40
GCH = ((0, 384),)
NG = len(GCH)
CH = ((0, 384),)
NCH = len(CH)


MSG = 96
MSG2 = 64
SPAN = 125.0


def encode(values, size):
    n, w = values.shape
    tiles = values.reshape(n // 8, 8, w)
    top = jnp.max(jnp.abs(tiles), axis=0) * 1.01 + 1e-30
    top = top.astype(jnp.bfloat16).astype(jnp.float32)
    code = jnp.exp2(tiles * (SPAN / top)[None]).reshape(n, w)
    return jnp.concatenate([code] + [top] * ((size - n) // 8), 0).astype(jnp.bfloat16)


def decode(message, n):
    wide = message.astype(jnp.float32)
    top = wide[n:n + 8] * (1.0 / SPAN)
    w = wide.shape[1]
    return (jnp.log2(wide[0:n]).reshape(n // 8, 8, w) * top[None]).reshape(n, w)


def kernel(
    x_hbm, cot_hbm, w_hbm, gain_ref, shift_ref, ig_ref, fin,
    x_own, x_send, x_all, cot, wv, gb, stat, normed_s, dsil_s, lcat, prod, part,
    ig_send, ig_recv, out_b, in_b, res1, fout_b, fin_b, res2,
    loc_sem, cs_send, cs_recv, xs_send, xs_recv, is_send, is_recv, r_send, r_recv, f_send, f_recv,
):
    clip, tm, rows = lax.axis_index("clip"), lax.axis_index("tm"), lax.axis_index("rows")
    x_hi, core = tm // 2, tm % 2
    j = tm * 2 + rows
    yy, zz = clip // 4, clip % 4

    def dev(tm_, rows_):
        return (clip, tm_, rows_)

    def ring(tm_, rows_, step):
        hi, co = tm_ // 2, tm_ % 2
        x = (hi * 2 + rows_ + step + 4) % 4
        return (x // 2) * 2 + co, x % 2

    rt, rr = ring(tm, rows, 1)
    lt, lr = ring(tm, rows, -1)
    ot, orow = ring(tm, rows, 2)
    sib_tm = x_hi * 2 + (1 - core)

    x_in = pltpu.make_async_copy(x_hbm, x_own, loc_sem.at[0])
    x_in.start()
    own_slot = pl.ds(pl.multiple_of(tm * OWN, OWN), OWN)
    c_in = []
    for c in range(NG):
        copy = pltpu.make_async_copy(
            cot_hbm.at[:, pl.ds(*GCH[c])], cot.at[rows, own_slot, pl.ds(*GCH[c])], loc_sem.at[4 + c]
        )
        copy.start()
        c_in.append(copy)
    w_in = pltpu.make_async_copy(
        w_hbm.at[:, pl.ds(pl.multiple_of(j * SL, SL), SL)], wv, loc_sem.at[2]
    )
    w_in.start()

    yp, ym = ((yy + 1) % 4) * 4 + zz, ((yy + 3) % 4) * 4 + zz
    yo, zo = ((yy + 2) % 4) * 4 + zz, yy * 4 + (zz + 2) % 4
    zp, zm = yy * 4 + (zz + 1) % 4, yy * 4 + (zz + 3) % 4
    barrier = pltpu.get_barrier_semaphore()
    for k in range(1, 8):
        p = (j + k) % 8
        pl.semaphore_signal(barrier, inc=1, device_id=dev(p // 2, p % 2), device_id_type=MESH)
    for other in (yp, ym, zp, zm):
        pl.semaphore_signal(barrier, inc=1, device_id=(other, tm, rows), device_id_type=MESH)

    x_in.wait()
    x_send[...] = x_own[...].astype(jnp.float32).T.astype(jnp.bfloat16)
    gb[0] = jnp.broadcast_to(gain_ref[...].reshape(1, C), (128, C)).T
    gb[1] = jnp.broadcast_to(shift_ref[...].reshape(1, C), (128, C)).T
    for h in range(2):
        cot[h, POS:, :] = jnp.zeros((OWN, C), jnp.bfloat16)
    pl.semaphore_wait(barrier, 11)

    def frame(tm_, f):
        return pl.ds(pl.multiple_of(tm_ * OWN + f * 128, 128), 128)

    def cot_copy(ch, slot, where, to):
        ref = cot.at[where[0], where[1], pl.ds(*GCH[ch])]
        return pltpu.make_async_remote_copy(
            src_ref=ref, dst_ref=ref,
            send_sem=cs_send.at[ch, slot], recv_sem=cs_recv.at[ch, slot],
            device_id=dev(*to), device_id_type=MESH,
        )

    right, left, sib = (rt, rr), (lt, lr), (sib_tm, rows)
    sends = []

    def send(ch, slot, where, to):
        copy = cot_copy(ch, slot, where, to)
        copy.start()
        sends.append(copy)

    def arrived(ch, slot, where):
        cot_copy(ch, slot, where, right).wait_recv()

    def whole(who):
        return who[1], pl.ds(pl.multiple_of(who[0] * OWN, OWN), OWN)

    def sib_of(who):
        return whole((who[0] + 1 - 2 * (who[0] % 2), who[1]))

    def own(ch):
        c_in[ch].wait()
        send(ch, 0, (rows, frame(tm, 0)), right)
        send(ch, 2, (rows, frame(tm, 1)), left)

    def own_rest(ch):
        send(ch, 1, (rows, frame(tm, 1)), right)
        send(ch, 3, (rows, frame(tm, 0)), left)
        send(ch, 4, (rows, own_slot), sib)

    def fwd1(ch):
        arrived(ch, 0, (lr, frame(lt, 0)))
        send(ch, 5, (lr, frame(lt, 0)), right)
        arrived(ch, 2, (rr, frame(rt, 1)))
        send(ch, 6, (rr, frame(rt, 1)), left)

    def fwd2(ch):
        arrived(ch, 1, (lr, frame(lt, 1)))
        send(ch, 7, whole((lt, lr)), sib)
        arrived(ch, 3, (rr, frame(rt, 0)))
        send(ch, 8, whole((rt, rr)), sib)

    def fwd3(ch):
        arrived(ch, 5, (orow, frame(ot, 0)))
        arrived(ch, 6, (orow, frame(ot, 1)))
        send(ch, 9, whole((ot, orow)), sib)

    def gathered_near(ch):
        arrived(ch, 4, sib_of((tm, rows)))
        arrived(ch, 7, sib_of((lt, lr)))
        arrived(ch, 8, sib_of((rt, rr)))

    def gathered_far(ch):
        arrived(ch, 9, sib_of((ot, orow)))

    own(0)

    own_lanes = pl.ds(pl.multiple_of(rows * POS + tm * OWN, OWN), OWN)
    x_self = pltpu.make_async_copy(
        x_send.at[pl.ds(pl.multiple_of(j * SL, SL), SL)], x_all.at[:, own_lanes], loc_sem.at[3]
    )
    x_self.start()
    xs = []
    for k in range(1, 8):
        p = (j + k) % 8
        c = pltpu.make_async_remote_copy(
            src_ref=x_send.at[pl.ds(pl.multiple_of(p * SL, SL), SL)], dst_ref=x_all.at[:, own_lanes],
            send_sem=xs_send.at[k - 1], recv_sem=xs_recv.at[k - 1],
            device_id=dev(p // 2, p % 2), device_id_type=MESH,
        )
        c.start()
        xs.append(c)

    mine = pl.ds(pl.multiple_of(j * SL, SL), SL)
    gain_l, shift_l = gb[0, mine, :], gb[1, mine, :]

    own_rest(0)
    fwd1(0)

    me = clip * 8 + j
    jobs = []
    for a in range(2):
        far, near = ((yy, zz), (zz, yy))[a]
        again = []
        for i in range(6):
            loc = (21, 19)[a] * far + 5 * near + i
            n = loc // 6
            tap = 2 * n if a == 0 else sum(jnp.where(n == k, t, 0) for k, t in enumerate(ODD))
            r = loc % 6
            tile = tap * 48 + 6 * j + r
            c_to, u = tile // 81, tile % 81
            j_to = jnp.minimum(u // 10, 7)
            if i < 4:
                ok = jnp.bool_(True)
            elif a == 0:
                ok = jnp.logical_or(i < 5, near == 3)
            elif i == 4:
                ok = jnp.logical_or(near < 3, far == 3)
            else:
                ok = jnp.logical_and(near == 3, far == 3)
            jobs.append((ok, c_to * 8 + j_to, u - 10 * j_to))
            edge = jnp.logical_and(u - 10 * j_to == 0, j_to > 0)
            again.append((jnp.logical_and(ok, edge), c_to * 8 + jnp.maximum(j_to - 1, 0), 10))
        jobs += again

    x_self.wait()
    for c in xs:
        c.wait_recv()

    row_g = lax.broadcasted_iota(jnp.int32, (SL, SL), 0)
    col_g = lax.broadcasted_iota(jnp.int32, (SL, SL), 1)

    def group_of(i):
        return sum((i >= PG * k).astype(jnp.int32) for k in (1, 2, 3))

    same = (group_of(row_g) == group_of(col_g)).astype(jnp.float32)

    def group_mean(values):
        total = jnp.sum(values, axis=1, keepdims=True)
        return jnp.dot(
            same, jnp.broadcast_to(total, (SL, 128)), precision=lax.Precision.HIGHEST,
            preferred_element_type=jnp.float32,
        ) * (1.0 / CELLS)

    s1 = jnp.zeros((SL, 128), jnp.float32)
    s2 = jnp.zeros((SL, 128), jnp.float32)
    for b in range(16):
        v = x_all[:, b * 128:(b + 1) * 128].astype(jnp.float32)
        s1 = s1 + v
        s2 = s2 + v * v
    mean = group_mean(s1)
    rstd = lax.rsqrt(group_mean(s2) - mean * mean + EPS)
    stat[...] = rstd

    lane = lax.broadcasted_iota(jnp.int32, (SL, 128), 1)
    for h in range(2):
        for dt in range(2):
            for dw in range(3):
                r0 = h * 432 + (dt * 3 + dw) * SL
                lcat[r0:r0 + SL, 0:(2 - dt) * 128] = jnp.zeros((SL, (2 - dt) * 128), jnp.bfloat16)
        for t in range(8):
            b = h * 8 + t
            sl = slice(b * 128, (b + 1) * 128)
            v = x_all[:, sl].astype(jnp.float32)
            normed = (v - mean) * rstd
            pre = normed * gain_l + shift_l
            s = 1.0 / (1.0 + jnp.exp(-pre))
            act = pre * s
            normed_s[:, sl] = normed
            dsil_s[:, sl] = s * (1.0 + pre * (1.0 - s)) * gain_l
            before = jnp.where(lane == 0, 0.0, pltpu.roll(act, 1, 1))
            after = jnp.where(lane == 127, 0.0, pltpu.roll(act, 127, 1))
            for dw, a in ((0, before), (1, act), (2, after)):
                a = a.astype(jnp.bfloat16)
                for dt in range(3):
                    t_out = t + 2 - dt
                    if t_out < 8:
                        r0 = h * 432 + (dt * 3 + dw) * SL
                        lcat[r0:r0 + SL, t_out * 128:(t_out + 1) * 128] = a

    half = POS // 2
    near_k = pl.ds(pl.multiple_of(x_hi * half, half), half)
    far_k = pl.ds(pl.multiple_of((1 - x_hi) * half, half), half)

    def weight_grad_near():
        prod[1 - rows] = jnp.dot(lcat[...], cot[1 - rows, 0:POS, :], preferred_element_type=jnp.float32)

    def weight_grad_far():
        prod[rows] = jnp.dot(lcat[:, near_k], cot[rows, near_k, :], preferred_element_type=jnp.float32)
        gathered_far(0)
        prod[rows] += jnp.dot(lcat[:, far_k], cot[rows, far_k, :], preferred_element_type=jnp.float32)
        for dt in range(3):
            for dw in range(3):
                q = (dt * 3 + dw) * SL
                near = [prod[r, k:k + SL] for r in range(2) for k in (q, q + 432)]
                for dh, v in ((0, near[2]), (1, near[0] + near[3]), (2, near[1])):
                    r0 = ORDER.index(dt * 9 + dh * 3 + dw) * SL
                    part[r0:r0 + SL] = v

    def ring_copy(ch, slot, src, dst, to):
        return pltpu.make_async_remote_copy(
            src_ref=src, dst_ref=dst, send_sem=r_send.at[ch, slot], recv_sem=r_recv.at[ch, slot],
            device_id=(to, tm, rows), device_id_type=MESH,
        )

    class Ring:
        def __init__(self, ch, slot, src, base, hop, pos, plus, minus, out_b, in_b, out):
            self.src, self.out, self.out_b, self.in_b = src, out, out_b, in_b

            def at(k, lo, hi):
                return pl.ds(pl.multiple_of(base + ((pos + k) % 4) * hop + lo, 8), hi - lo)

            self.at = at
            self.all = [
                ring_copy(ch, slot + k, out_b.at[k], in_b.at[k], minus if k % 2 else plus) for k in range(6)
            ]

        def put(self, k, values):
            self.out_b[k] = encode(values, MSG)
            self.all[k].start()

        def got(self, k, n):
            self.all[k].wait_recv()
            return decode(self.in_b[k], n)

        def start(self):
            self.put(0, self.src[self.at(2, 0, CUT1), :])
            self.put(1, self.src[self.at(2, CUT1, WIN1), :])

        def near(self):
            self.put(2, self.src[self.at(1, CUT1, WIN1), :])
            self.put(3, self.src[self.at(3, 0, CUT1), :])

        def middle(self):
            self.put(4, self.got(0, CUT1) + self.src[self.at(1, 0, CUT1), :])
            self.put(5, self.got(1, WIN1 - CUT1) + self.src[self.at(3, CUT1, WIN1), :])

        def end(self):
            self.out[0:CUT1] = self.src[self.at(0, 0, CUT1), :] + self.got(3, CUT1) + self.got(4, CUT1)
            self.out[CUT1:WIN1] = (
                self.src[self.at(0, CUT1, WIN1), :] + self.got(2, WIN1 - CUT1) + self.got(5, WIN1 - CUT1)
            )

    class Direct:
        def __init__(self, ch, slot, src, pos, to, out_b, in_b, out):
            self.src, self.out_b, self.in_b, self.out = src, out_b, in_b, out
            self.at = [pl.ds(pl.multiple_of(((pos + k) % 4) * HOP2, 8), WIN2) for k in range(4)]
            self.all = [ring_copy(ch, slot + k, out_b.at[k], in_b.at[k], to[k]) for k in range(3)]

        def start(self):
            for k in (1, 0, 2):
                self.out_b[k] = encode(self.src[self.at[k + 1], :], MSG2)
                self.all[k].start()

        def end(self):
            total = self.src[self.at[0], :]
            for k in (0, 2, 1):
                self.all[k].wait_recv()
                total = total + decode(self.in_b[k], WIN2)
            self.out[...] = total

    first, second = [], []
    for c in range(NCH):
        for a in range(2):
            lanes = pl.ds(*CH[c])
            along = ((yy, yp, ym, yo), (zz, zp, zm, zo))
            pos1, plus1, minus1, _ = along[a]
            pos2, plus2, minus2, far2 = along[1 - a]
            first.append(Ring(
                c, a * 6, part.at[:, lanes], BASES[a], HOPS[a], pos1, plus1, minus1,
                out_b.at[a, :, :, lanes], in_b.at[a, :, :, lanes], res1.at[a, :, lanes],
            ))
            second.append(Direct(
                c, 12 + a * 3, res1.at[a, :, lanes], pos2, (plus2, far2, minus2),
                fout_b.at[a, :, :, lanes], fin_b.at[a, :, :, lanes], res2.at[a, :, lanes],
            ))

    def start1(ch):
        for st in first[2 * ch:2 * ch + 2]:
            st.start()

    def near1(ch):
        for st in first[2 * ch:2 * ch + 2]:
            st.near()

    def mid1(ch):
        for st in first[2 * ch:2 * ch + 2]:
            st.middle()

    def turn(ch):
        for st, nxt in zip(first[2 * ch:2 * ch + 2], second[2 * ch:2 * ch + 2]):
            st.end()
            nxt.start()

    def end2(ch):
        for a in range(2):
            second[2 * ch + a].end()
            scatter(ch, begin, a * 12, a * 12 + 12)

    nt = (((1,), (1,)), ((), ()))
    grads, cots = [], []

    def grad_active(h):
        acc = jnp.zeros((144, POS), jnp.float32)
        for hs in range(2):
            dh = h - hs + 1
            for dt in range(3):
                tap = dt * 9 + dh * 3
                w_rows = wv[tap:tap + 3].reshape(144, C)
                c_rows = cot[hs, (2 - dt) * 128:(2 - dt) * 128 + POS, :]
                if hs == h and dt == 2:
                    both = lax.dot_general(
                        jnp.concatenate([w_rows, pick], 0), c_rows, nt, preferred_element_type=jnp.float32
                    )
                    cots.append(both[144:192])
                    acc = acc + both[0:144]
                else:
                    acc = acc + lax.dot_general(w_rows, c_rows, nt, preferred_element_type=jnp.float32)
        grads.append(acc)

    def input_grad():
        t1 = jnp.zeros((SL, 128), jnp.float32)
        t2 = jnp.zeros((SL, 128), jnp.float32)
        for h in range(2):
            for t in range(8):
                sl = slice(t * 128, (t + 1) * 128)
                gl = slice((h * 8 + t) * 128, (h * 8 + t + 1) * 128)
                g0, g1, g2 = (grads[h][k * SL:(k + 1) * SL, sl] for k in range(3))
                g = (
                    g1
                    + jnp.where(lane == 127, 0.0, pltpu.roll(g0, 127, 1))
                    + jnp.where(lane == 0, 0.0, pltpu.roll(g2, 1, 1))
                )
                gn = g * dsil_s[:, gl]
                dsil_s[:, gl] = gn
                t1 = t1 + gn
                t2 = t2 + gn * normed_s[:, gl]
        m1, m2 = group_mean(t1), group_mean(t2)
        rstd_l = stat[...]
        for h in range(2):
            for t in range(8):
                sl = slice(t * 128, (t + 1) * 128)
                gl = slice((h * 8 + t) * 128, (h * 8 + t + 1) * 128)
                out = cots[h][:, sl] + rstd_l * (dsil_s[:, gl] - m1 - normed_s[:, gl] * m2)
                ig_send[:, gl] = out.astype(jnp.bfloat16)

    ig_self = pltpu.make_async_copy(ig_send.at[:, own_lanes], ig_recv.at[mine], loc_sem.at[3])
    igs = []
    for k in range(1, 8):
        p = (j + k) % 8
        lanes = pl.ds(pl.multiple_of((p % 2) * POS + (p // 2) * OWN, OWN), OWN)
        igs.append(pltpu.make_async_remote_copy(
            src_ref=ig_send.at[:, lanes], dst_ref=ig_recv.at[mine],
            send_sem=is_send.at[k - 1], recv_sem=is_recv.at[k - 1],
            device_id=dev(p // 2, p % 2), device_id_type=MESH,
        ))

    def ig_out():
        ig_self.wait()
        for c in igs:
            c.wait_recv()
        ig_ref[...] = ig_recv[...].astype(jnp.float32).T.astype(jnp.bfloat16)

    def scatter(ch, act, lo=0, hi=24):
        for n in range(lo, hi):
            ok, d_to, slot = jobs[n]
            src = res2.at[n // 12, pl.ds(n % 6 * 8, 8), pl.ds(*CH[ch])]
            act(ch, n, ok, src, d_to, slot)

    def fin_at(ch, slot):
        return fin.at[pl.ds(pl.multiple_of(slot * 8, 8), 8), pl.ds(*CH[ch])]

    def fin_copy(ch, n, src, d_to, slot):
        return pltpu.make_async_remote_copy(
            src_ref=src, dst_ref=fin_at(ch, slot), send_sem=f_send.at[ch, n], recv_sem=f_recv.at[ch],
            device_id=(d_to // 8, d_to % 8 // 2, d_to % 2), device_id_type=MESH,
        )

    def begin(ch, n, ok, src, d_to, slot):
        @pl.when(jnp.logical_and(ok, d_to == me))
        def _():
            pltpu.make_async_copy(src, fin_at(ch, slot), f_recv.at[ch]).start()

        @pl.when(jnp.logical_and(ok, d_to != me))
        def _():
            fin_copy(ch, n, src, d_to, slot).start()

    def finish(ch, n, ok, src, d_to, slot):
        @pl.when(jnp.logical_and(ok, d_to != me))
        def _():
            fin_copy(ch, n, src, d_to, slot).wait_send()

    fwd2(0)
    gathered_near(0)
    weight_grad_near()
    fwd3(0)
    weight_grad_far()
    start1(0)
    near1(0)
    w_in.wait()
    pick = (
        lax.broadcasted_iota(jnp.int32, (SL, C), 1)
        == lax.broadcasted_iota(jnp.int32, (SL, C), 0) + j * SL
    ).astype(jnp.bfloat16)
    grad_active(0)
    grad_active(1)
    mid1(0)
    input_grad()
    for c in [ig_self] + igs:
        c.start()
    turn(0)
    ig_out()
    end2(0)

    for c in sends + xs + igs:
        c.wait_send()
    for st in first + second:
        for c in st.all:
            c.wait_send()
    for c in range(NCH):
        lanes = fin.at[:, pl.ds(*CH[c])]
        pltpu.make_async_copy(lanes, lanes, f_recv.at[c]).wait()
    for c in range(NCH):
        scatter(c, finish)


def write_out(ig_in, fin, ig_out, wg_out, sem):
    copy = pltpu.make_async_copy(ig_in, ig_out, sem)
    copy.start()
    j = lax.axis_index("tm") * 2 + lax.axis_index("rows")
    for k in range(8):
        @pl.when(j == k)
        def _(k=k):
            wg_out[...] = fin[k:k + 81, :] * SCALE
    copy.wait()


def per_device(inputs, cotangent, weight, gain, shift_term):
    f32, bf16 = jnp.float32, jnp.bfloat16
    hbm = pl.BlockSpec(memory_space=pltpu.HBM)
    vmem = pl.BlockSpec(memory_space=pltpu.VMEM)
    dma = pltpu.SemaphoreType.DMA
    ig, fin = pl.pallas_call(
        kernel,
        out_shape=(pltpu.VMEM((OWN, C), bf16), pltpu.VMEM((88, C), f32)),
        in_specs=[hbm, hbm, hbm, vmem, vmem],
        out_specs=(vmem, vmem),
        scratch_shapes=[
            pltpu.VMEM((OWN, C), bf16),
            pltpu.VMEM((C, OWN), bf16),
            pltpu.VMEM((SL, 2 * POS), bf16),
            pltpu.VMEM((2, POS + OWN, C), bf16),
            pltpu.VMEM((27, SL, C), bf16),
            pltpu.VMEM((2, C, 128), f32),
            pltpu.VMEM((SL, 128), f32),
            pltpu.VMEM((SL, 2 * POS), f32),
            pltpu.VMEM((SL, 2 * POS), f32),
            pltpu.VMEM((864, POS), bf16),
            pltpu.VMEM((2, 864, C), f32),
            pltpu.VMEM((1296, C), f32),
            pltpu.VMEM((SL, 2 * POS), bf16),
            pltpu.VMEM((C, OWN), bf16),
            pltpu.VMEM((2, 6, MSG, C), bf16),
            pltpu.VMEM((2, 6, MSG, C), bf16),
            pltpu.VMEM((2, WIN1, C), f32),
            pltpu.VMEM((2, 3, MSG2, C), bf16),
            pltpu.VMEM((2, 3, MSG2, C), bf16),
            pltpu.VMEM((2, WIN2, C), f32),
            dma((4 + NG,)), dma((NG, 10)), dma((NG, 10)), dma((7,)), dma((7,)), dma((7,)), dma((7,)),
            dma((NCH, 18)), dma((NCH, 18)), dma((NCH, 24)), dma((NCH,)),
        ],
        compiler_params=pltpu.CompilerParams(
            collective_id=0, has_side_effects=True, vmem_limit_bytes=56 * 1024 * 1024
        ),
        name="resblock_backward",
    )(
        inputs.reshape(OWN, C),
        cotangent.reshape(OWN, C),
        weight.reshape(27, C, C),
        gain,
        shift_term,
    )
    ig, fin = (pltpu.with_memory_space_constraint(v, pltpu.VMEM) for v in (ig, fin))
    ig, wg = pl.pallas_call(
        write_out,
        out_shape=(
            jax.ShapeDtypeStruct((OWN, C), bf16),
            jax.ShapeDtypeStruct((81, C), f32),
        ),
        in_specs=[vmem, vmem],
        out_specs=(hbm, vmem),
        scratch_shapes=[dma],
        name="write_out",
    )(ig, fin)
    return ig.reshape(1, 2, 1, 128, C), wg


def solution(mesh):
    return jax.shard_map(
        per_device,
        mesh=mesh,
        in_specs=(
            P("clip", "tm", "rows", None, None),
            P("clip", "tm", "rows", None, None),
            P(),
            P(),
            P(),
        ),
        out_specs=(P("clip", "tm", "rows", None, None), P(("clip", "tm", "rows"), None)),
        check_vma=False,
    )
```

```python
import jax
import jax.numpy as jnp
from jax import lax
from jax.experimental import pallas as pl
from jax.experimental.pallas import tpu as pltpu
from jax.sharding import PartitionSpec as P

MESH = pl.DeviceIdType.MESH
C = 384
SL = 48
PG = 12
POS = 1024
OWN = 256
EPS = 1e-05
CELLS = 12 * 2048
SCALE = 1.0 / 128
ODD = (1, 7, 13, 21, 9, 15, 23, 3, 11, 17, 5, 19, 25)
ORDER = tuple(range(0, 27, 2)) + ODD
WIN1, CUT1 = 168, 88
BASES, HOPS = (0, 672), (168, 152)
WIN2, HOP2 = 48, 40
GCH = ((0, 384),)
NG = len(GCH)
CH = ((0, 384),)
NCH = len(CH)


MSG = 96
MSG2 = 64
SPAN = 125.0


def encode(values, size):
    n, w = values.shape
    tiles = values.reshape(n // 8, 8, w)
    top = jnp.max(jnp.abs(tiles), axis=0) * 1.01 + 1e-30
    top = top.astype(jnp.bfloat16).astype(jnp.float32)
    code = jnp.exp2(tiles * (SPAN / top)[None]).reshape(n, w)
    return jnp.concatenate([code] + [top] * ((size - n) // 8), 0).astype(jnp.bfloat16)


def decode(message, n):
    wide = message.astype(jnp.float32)
    top = wide[n:n + 8] * (1.0 / SPAN)
    w = wide.shape[1]
    return (jnp.log2(wide[0:n]).reshape(n // 8, 8, w) * top[None]).reshape(n, w)


def kernel(
    x_hbm, cot_hbm, w_hbm, gain_ref, shift_ref, ig_ref, fin,
    x_own, x_send, x_all, cot, wv, gb, stat, normed_s, dsil_s, lcat, prod, part,
    ig_send, ig_recv, out_b, in_b, res1, fout_b, fin_b, res2,
    loc_sem, cs_send, cs_recv, xs_send, xs_recv, is_send, is_recv, r_send, r_recv, f_send, f_recv,
):
    clip, tm, rows = lax.axis_index("clip"), lax.axis_index("tm"), lax.axis_index("rows")
    x_hi, core = tm // 2, tm % 2
    j = tm * 2 + rows
    yy, zz = clip // 4, clip % 4

    def dev(tm_, rows_):
        return (clip, tm_, rows_)

    def ring(tm_, rows_, step):
        hi, co = tm_ // 2, tm_ % 2
        x = (hi * 2 + rows_ + step + 4) % 4
        return (x // 2) * 2 + co, x % 2

    rt, rr = ring(tm, rows, 1)
    lt, lr = ring(tm, rows, -1)
    ot, orow = ring(tm, rows, 2)
    sib_tm = x_hi * 2 + (1 - core)

    yp, ym = ((yy + 1) % 4) * 4 + zz, ((yy + 3) % 4) * 4 + zz
    yo, zo = ((yy + 2) % 4) * 4 + zz, yy * 4 + (zz + 2) % 4
    zp, zm = yy * 4 + (zz + 1) % 4, yy * 4 + (zz + 3) % 4
    barrier = pltpu.get_barrier_semaphore()
    for k in range(1, 8):
        p = (j + k) % 8
        pl.semaphore_signal(barrier, inc=1, device_id=dev(p // 2, p % 2), device_id_type=MESH)
    for other in (yp, ym, zp, zm):
        pl.semaphore_signal(barrier, inc=1, device_id=(other, tm, rows), device_id_type=MESH)


    x_in = pltpu.make_async_copy(x_hbm, x_own, loc_sem.at[0])
    x_in.start()
    own_slot = pl.ds(pl.multiple_of(tm * OWN, OWN), OWN)
    c_in = []
    for c in range(NG):
        copy = pltpu.make_async_copy(
            cot_hbm.at[:, pl.ds(*GCH[c])], cot.at[rows, own_slot, pl.ds(*GCH[c])], loc_sem.at[4 + c]
        )
        copy.start()
        c_in.append(copy)
    w_in = pltpu.make_async_copy(
        w_hbm.at[:, pl.ds(pl.multiple_of(j * SL, SL), SL)], wv, loc_sem.at[2]
    )
    w_in.start()

    pl.semaphore_wait(barrier, 11)

    def frame(tm_, f):
        return pl.ds(pl.multiple_of(tm_ * OWN + f * 128, 128), 128)

    def cot_copy(ch, slot, where, to):
        ref = cot.at[where[0], where[1], pl.ds(*GCH[ch])]
        return pltpu.make_async_remote_copy(
            src_ref=ref, dst_ref=ref,
            send_sem=cs_send.at[ch, slot], recv_sem=cs_recv.at[ch, slot],
            device_id=dev(*to), device_id_type=MESH,
        )

    right, left, sib = (rt, rr), (lt, lr), (sib_tm, rows)
    sends = []

    def send(ch, slot, where, to):
        copy = cot_copy(ch, slot, where, to)
        copy.start()
        sends.append(copy)

    def arrived(ch, slot, where):
        cot_copy(ch, slot, where, right).wait_recv()

    def whole(who):
        return who[1], pl.ds(pl.multiple_of(who[0] * OWN, OWN), OWN)

    def sib_of(who):
        return whole((who[0] + 1 - 2 * (who[0] % 2), who[1]))

    def own(ch):
        c_in[ch].wait()
        send(ch, 0, (rows, frame(tm, 0)), right)
        send(ch, 2, (rows, frame(tm, 1)), left)

    def own_rest(ch):
        send(ch, 1, (rows, frame(tm, 1)), right)
        send(ch, 3, (rows, frame(tm, 0)), left)
        send(ch, 4, (rows, own_slot), sib)

    def fwd1(ch):
        arrived(ch, 0, (lr, frame(lt, 0)))
        send(ch, 5, (lr, frame(lt, 0)), right)
        arrived(ch, 2, (rr, frame(rt, 1)))
        send(ch, 6, (rr, frame(rt, 1)), left)

    def fwd2(ch):
        arrived(ch, 1, (lr, frame(lt, 1)))
        send(ch, 7, whole((lt, lr)), sib)
        arrived(ch, 3, (rr, frame(rt, 0)))
        send(ch, 8, whole((rt, rr)), sib)

    def fwd3(ch):
        arrived(ch, 5, (orow, frame(ot, 0)))
        arrived(ch, 6, (orow, frame(ot, 1)))
        send(ch, 9, whole((ot, orow)), sib)

    def gathered_near(ch):
        arrived(ch, 4, sib_of((tm, rows)))
        arrived(ch, 7, sib_of((lt, lr)))
        arrived(ch, 8, sib_of((rt, rr)))

    def gathered_far(ch):
        arrived(ch, 9, sib_of((ot, orow)))

    own(0)

    x_in.wait()
    x_send[...] = x_own[...].astype(jnp.float32).T.astype(jnp.bfloat16)
    own_lanes = pl.ds(pl.multiple_of(rows * POS + tm * OWN, OWN), OWN)
    x_self = pltpu.make_async_copy(
        x_send.at[pl.ds(pl.multiple_of(j * SL, SL), SL)], x_all.at[:, own_lanes], loc_sem.at[3]
    )
    x_self.start()
    xs = []
    for k in range(1, 8):
        p = (j + k) % 8
        c = pltpu.make_async_remote_copy(
            src_ref=x_send.at[pl.ds(pl.multiple_of(p * SL, SL), SL)], dst_ref=x_all.at[:, own_lanes],
            send_sem=xs_send.at[k - 1], recv_sem=xs_recv.at[k - 1],
            device_id=dev(p // 2, p % 2), device_id_type=MESH,
        )
        c.start()
        xs.append(c)

    own_rest(0)

    gb[0] = jnp.broadcast_to(gain_ref[...].reshape(1, C), (128, C)).T
    gb[1] = jnp.broadcast_to(shift_ref[...].reshape(1, C), (128, C)).T
    for h in range(2):
        cot[h, POS:, :] = jnp.zeros((OWN, C), jnp.bfloat16)
    mine = pl.ds(pl.multiple_of(j * SL, SL), SL)
    gain_l, shift_l = gb[0, mine, :], gb[1, mine, :]

    fwd1(0)

    me = clip * 8 + j
    jobs = []
    for a in range(2):
        far, near = ((yy, zz), (zz, yy))[a]
        again = []
        for i in range(6):
            loc = (21, 19)[a] * far + 5 * near + i
            n = loc // 6
            tap = 2 * n if a == 0 else sum(jnp.where(n == k, t, 0) for k, t in enumerate(ODD))
            r = loc % 6
            tile = tap * 48 + 6 * j + r
            c_to, u = tile // 81, tile % 81
            j_to = jnp.minimum(u // 10, 7)
            if i < 4:
                ok = jnp.bool_(True)
            elif a == 0:
                ok = jnp.logical_or(i < 5, near == 3)
            elif i == 4:
                ok = jnp.logical_or(near < 3, far == 3)
            else:
                ok = jnp.logical_and(near == 3, far == 3)
            jobs.append((ok, c_to * 8 + j_to, u - 10 * j_to))
            edge = jnp.logical_and(u - 10 * j_to == 0, j_to > 0)
            again.append((jnp.logical_and(ok, edge), c_to * 8 + jnp.maximum(j_to - 1, 0), 10))
        jobs += again

    x_self.wait()
    for c in xs:
        c.wait_recv()

    row_g = lax.broadcasted_iota(jnp.int32, (SL, SL), 0)
    col_g = lax.broadcasted_iota(jnp.int32, (SL, SL), 1)

    def group_of(i):
        return sum((i >= PG * k).astype(jnp.int32) for k in (1, 2, 3))

    same = (group_of(row_g) == group_of(col_g)).astype(jnp.float32)

    def group_mean(values):
        total = jnp.sum(values, axis=1, keepdims=True)
        return jnp.dot(
            same, jnp.broadcast_to(total, (SL, 128)), precision=lax.Precision.HIGHEST,
            preferred_element_type=jnp.float32,
        ) * (1.0 / CELLS)

    s1 = jnp.zeros((SL, 128), jnp.float32)
    s2 = jnp.zeros((SL, 128), jnp.float32)
    for b in range(16):
        v = x_all[:, b * 128:(b + 1) * 128].astype(jnp.float32)
        s1 = s1 + v
        s2 = s2 + v * v
    mean = group_mean(s1)
    rstd = lax.rsqrt(group_mean(s2) - mean * mean + EPS)
    stat[...] = rstd

    lane = lax.broadcasted_iota(jnp.int32, (SL, 128), 1)
    for h in range(2):
        for dt in range(2):
            for dw in range(3):
                r0 = h * 432 + (dt * 3 + dw) * SL
                lcat[r0:r0 + SL, 0:(2 - dt) * 128] = jnp.zeros((SL, (2 - dt) * 128), jnp.bfloat16)
        for t in range(8):
            b = h * 8 + t
            sl = slice(b * 128, (b + 1) * 128)
            v = x_all[:, sl].astype(jnp.float32)
            normed = (v - mean) * rstd
            pre = normed * gain_l + shift_l
            s = 1.0 / (1.0 + jnp.exp(-pre))
            act = pre * s
            normed_s[:, sl] = normed
            dsil_s[:, sl] = s * (1.0 + pre * (1.0 - s)) * gain_l
            before = jnp.where(lane == 0, 0.0, pltpu.roll(act, 1, 1))
            after = jnp.where(lane == 127, 0.0, pltpu.roll(act, 127, 1))
            for dw, a in ((0, before), (1, act), (2, after)):
                a = a.astype(jnp.bfloat16)
                for dt in range(3):
                    t_out = t + 2 - dt
                    if t_out < 8:
                        r0 = h * 432 + (dt * 3 + dw) * SL
                        lcat[r0:r0 + SL, t_out * 128:(t_out + 1) * 128] = a

    half = POS // 2
    near_k = pl.ds(pl.multiple_of(x_hi * half, half), half)
    far_k = pl.ds(pl.multiple_of((1 - x_hi) * half, half), half)

    def weight_grad_near():
        prod[1 - rows] = jnp.dot(lcat[...], cot[1 - rows, 0:POS, :], preferred_element_type=jnp.float32)

    def weight_grad_far():
        prod[rows] = jnp.dot(lcat[:, near_k], cot[rows, near_k, :], preferred_element_type=jnp.float32)
        gathered_far(0)
        prod[rows] += jnp.dot(lcat[:, far_k], cot[rows, far_k, :], preferred_element_type=jnp.float32)
        for dt in range(3):
            for dw in range(3):
                q = (dt * 3 + dw) * SL
                near = [prod[r, k:k + SL] for r in range(2) for k in (q, q + 432)]
                for dh, v in ((0, near[2]), (1, near[0] + near[3]), (2, near[1])):
                    r0 = ORDER.index(dt * 9 + dh * 3 + dw) * SL
                    part[r0:r0 + SL] = v

    def ring_copy(ch, slot, src, dst, to):
        return pltpu.make_async_remote_copy(
            src_ref=src, dst_ref=dst, send_sem=r_send.at[ch, slot], recv_sem=r_recv.at[ch, slot],
            device_id=(to, tm, rows), device_id_type=MESH,
        )

    class Ring:
        def __init__(self, ch, slot, src, base, hop, pos, plus, minus, out_b, in_b, out):
            self.src, self.out, self.out_b, self.in_b = src, out, out_b, in_b

            def at(k, lo, hi):
                return pl.ds(pl.multiple_of(base + ((pos + k) % 4) * hop + lo, 8), hi - lo)

            self.at = at
            self.all = [
                ring_copy(ch, slot + k, out_b.at[k], in_b.at[k], minus if k % 2 else plus) for k in range(6)
            ]

        def put(self, k, values):
            self.out_b[k] = encode(values, MSG)
            self.all[k].start()

        def got(self, k, n):
            self.all[k].wait_recv()
            return decode(self.in_b[k], n)

        def start(self):
            self.put(0, self.src[self.at(2, 0, CUT1), :])
            self.put(1, self.src[self.at(2, CUT1, WIN1), :])

        def near(self):
            self.put(2, self.src[self.at(1, CUT1, WIN1), :])
            self.put(3, self.src[self.at(3, 0, CUT1), :])

        def middle(self):
            self.put(4, self.got(0, CUT1) + self.src[self.at(1, 0, CUT1), :])
            self.put(5, self.got(1, WIN1 - CUT1) + self.src[self.at(3, CUT1, WIN1), :])

        def end(self):
            self.out[0:CUT1] = self.src[self.at(0, 0, CUT1), :] + self.got(3, CUT1) + self.got(4, CUT1)
            self.out[CUT1:WIN1] = (
                self.src[self.at(0, CUT1, WIN1), :] + self.got(2, WIN1 - CUT1) + self.got(5, WIN1 - CUT1)
            )

    class Direct:
        def __init__(self, ch, slot, src, pos, to, out_b, in_b, out):
            self.src, self.out_b, self.in_b, self.out = src, out_b, in_b, out
            self.at = [pl.ds(pl.multiple_of(((pos + k) % 4) * HOP2, 8), WIN2) for k in range(4)]
            self.all = [ring_copy(ch, slot + k, out_b.at[k], in_b.at[k], to[k]) for k in range(3)]

        def start(self):
            for k in (1, 0, 2):
                self.out_b[k] = encode(self.src[self.at[k + 1], :], MSG2)
                self.all[k].start()

        def end(self):
            total = self.src[self.at[0], :]
            for k in (0, 2, 1):
                self.all[k].wait_recv()
                total = total + decode(self.in_b[k], WIN2)
            self.out[...] = total

    first, second = [], []
    for c in range(NCH):
        for a in range(2):
            lanes = pl.ds(*CH[c])
            along = ((yy, yp, ym, yo), (zz, zp, zm, zo))
            pos1, plus1, minus1, _ = along[a]
            pos2, plus2, minus2, far2 = along[1 - a]
            first.append(Ring(
                c, a * 6, part.at[:, lanes], BASES[a], HOPS[a], pos1, plus1, minus1,
                out_b.at[a, :, :, lanes], in_b.at[a, :, :, lanes], res1.at[a, :, lanes],
            ))
            second.append(Direct(
                c, 12 + a * 3, res1.at[a, :, lanes], pos2, (plus2, far2, minus2),
                fout_b.at[a, :, :, lanes], fin_b.at[a, :, :, lanes], res2.at[a, :, lanes],
            ))

    def start1(ch):
        for st in first[2 * ch:2 * ch + 2]:
            st.start()

    def near1(ch):
        for st in first[2 * ch:2 * ch + 2]:
            st.near()

    def mid1(ch):
        for st in first[2 * ch:2 * ch + 2]:
            st.middle()

    def turn(ch):
        for st, nxt in zip(first[2 * ch:2 * ch + 2], second[2 * ch:2 * ch + 2]):
            st.end()
            nxt.start()

    def end2(ch):
        for a in range(2):
            second[2 * ch + a].end()
            scatter(ch, begin, a * 12, a * 12 + 12)

    nt = (((1,), (1,)), ((), ()))
    grads, cots = [], []

    def grad_active(h):
        acc = jnp.zeros((144, POS), jnp.float32)
        for hs in range(2):
            dh = h - hs + 1
            for dt in range(3):
                tap = dt * 9 + dh * 3
                w_rows = wv[tap:tap + 3].reshape(144, C)
                c_rows = cot[hs, (2 - dt) * 128:(2 - dt) * 128 + POS, :]
                if hs == h and dt == 2:
                    both = lax.dot_general(
                        jnp.concatenate([w_rows, pick], 0), c_rows, nt, preferred_element_type=jnp.float32
                    )
                    cots.append(both[144:192])
                    acc = acc + both[0:144]
                else:
                    acc = acc + lax.dot_general(w_rows, c_rows, nt, preferred_element_type=jnp.float32)
        grads.append(acc)

    def input_grad():
        t1 = jnp.zeros((SL, 128), jnp.float32)
        t2 = jnp.zeros((SL, 128), jnp.float32)
        for h in range(2):
            for t in range(8):
                sl = slice(t * 128, (t + 1) * 128)
                gl = slice((h * 8 + t) * 128, (h * 8 + t + 1) * 128)
                g0, g1, g2 = (grads[h][k * SL:(k + 1) * SL, sl] for k in range(3))
                g = (
                    g1
                    + jnp.where(lane == 127, 0.0, pltpu.roll(g0, 127, 1))
                    + jnp.where(lane == 0, 0.0, pltpu.roll(g2, 1, 1))
                )
                gn = g * dsil_s[:, gl]
                dsil_s[:, gl] = gn
                t1 = t1 + gn
                t2 = t2 + gn * normed_s[:, gl]
        m1, m2 = group_mean(t1), group_mean(t2)
        rstd_l = stat[...]
        for h in range(2):
            for t in range(8):
                sl = slice(t * 128, (t + 1) * 128)
                gl = slice((h * 8 + t) * 128, (h * 8 + t + 1) * 128)
                out = cots[h][:, sl] + rstd_l * (dsil_s[:, gl] - m1 - normed_s[:, gl] * m2)
                ig_send[:, gl] = out.astype(jnp.bfloat16)

    ig_self = pltpu.make_async_copy(ig_send.at[:, own_lanes], ig_recv.at[mine], loc_sem.at[3])
    igs = []
    for k in range(1, 8):
        p = (j + k) % 8
        lanes = pl.ds(pl.multiple_of((p % 2) * POS + (p // 2) * OWN, OWN), OWN)
        igs.append(pltpu.make_async_remote_copy(
            src_ref=ig_send.at[:, lanes], dst_ref=ig_recv.at[mine],
            send_sem=is_send.at[k - 1], recv_sem=is_recv.at[k - 1],
            device_id=dev(p // 2, p % 2), device_id_type=MESH,
        ))

    def ig_out():
        ig_self.wait()
        for c in igs:
            c.wait_recv()
        ig_ref[...] = ig_recv[...].astype(jnp.float32).T.astype(jnp.bfloat16)

    def scatter(ch, act, lo=0, hi=24):
        for n in range(lo, hi):
            ok, d_to, slot = jobs[n]
            src = res2.at[n // 12, pl.ds(n % 6 * 8, 8), pl.ds(*CH[ch])]
            act(ch, n, ok, src, d_to, slot)

    def fin_at(ch, slot):
        return fin.at[pl.ds(pl.multiple_of(slot * 8, 8), 8), pl.ds(*CH[ch])]

    def fin_copy(ch, n, src, d_to, slot):
        return pltpu.make_async_remote_copy(
            src_ref=src, dst_ref=fin_at(ch, slot), send_sem=f_send.at[ch, n], recv_sem=f_recv.at[ch],
            device_id=(d_to // 8, d_to % 8 // 2, d_to % 2), device_id_type=MESH,
        )

    def begin(ch, n, ok, src, d_to, slot):
        @pl.when(jnp.logical_and(ok, d_to == me))
        def _():
            pltpu.make_async_copy(src, fin_at(ch, slot), f_recv.at[ch]).start()

        @pl.when(jnp.logical_and(ok, d_to != me))
        def _():
            fin_copy(ch, n, src, d_to, slot).start()

    def finish(ch, n, ok, src, d_to, slot):
        @pl.when(jnp.logical_and(ok, d_to != me))
        def _():
            fin_copy(ch, n, src, d_to, slot).wait_send()

    fwd2(0)
    gathered_near(0)
    weight_grad_near()
    fwd3(0)
    weight_grad_far()
    start1(0)
    near1(0)
    w_in.wait()
    pick = (
        lax.broadcasted_iota(jnp.int32, (SL, C), 1)
        == lax.broadcasted_iota(jnp.int32, (SL, C), 0) + j * SL
    ).astype(jnp.bfloat16)
    grad_active(0)
    grad_active(1)
    mid1(0)
    input_grad()
    for c in [ig_self] + igs:
        c.start()
    turn(0)
    end2(0)
    ig_out()

    for c in sends + xs + igs:
        c.wait_send()
    for st in first + second:
        for c in st.all:
            c.wait_send()
    for c in range(NCH):
        lanes = fin.at[:, pl.ds(*CH[c])]
        pltpu.make_async_copy(lanes, lanes, f_recv.at[c]).wait()
    for c in range(NCH):
        scatter(c, finish)


def write_out(ig_in, fin, ig_out, wg_out, sem):
    copy = pltpu.make_async_copy(ig_in, ig_out, sem)
    copy.start()
    j = lax.axis_index("tm") * 2 + lax.axis_index("rows")
    for k in range(8):
        @pl.when(j == k)
        def _(k=k):
            wg_out[...] = fin[k:k + 81, :] * SCALE
    copy.wait()


def per_device(inputs, cotangent, weight, gain, shift_term):
    f32, bf16 = jnp.float32, jnp.bfloat16
    hbm = pl.BlockSpec(memory_space=pltpu.HBM)
    vmem = pl.BlockSpec(memory_space=pltpu.VMEM)
    dma = pltpu.SemaphoreType.DMA
    ig, fin = pl.pallas_call(
        kernel,
        out_shape=(pltpu.VMEM((OWN, C), bf16), pltpu.VMEM((88, C), f32)),
        in_specs=[hbm, hbm, hbm, vmem, vmem],
        out_specs=(vmem, vmem),
        scratch_shapes=[
            pltpu.VMEM((OWN, C), bf16),
            pltpu.VMEM((C, OWN), bf16),
            pltpu.VMEM((SL, 2 * POS), bf16),
            pltpu.VMEM((2, POS + OWN, C), bf16),
            pltpu.VMEM((27, SL, C), bf16),
            pltpu.VMEM((2, C, 128), f32),
            pltpu.VMEM((SL, 128), f32),
            pltpu.VMEM((SL, 2 * POS), f32),
            pltpu.VMEM((SL, 2 * POS), f32),
            pltpu.VMEM((864, POS), bf16),
            pltpu.VMEM((2, 864, C), f32),
            pltpu.VMEM((1296, C), f32),
            pltpu.VMEM((SL, 2 * POS), bf16),
            pltpu.VMEM((C, OWN), bf16),
            pltpu.VMEM((2, 6, MSG, C), bf16),
            pltpu.VMEM((2, 6, MSG, C), bf16),
            pltpu.VMEM((2, WIN1, C), f32),
            pltpu.VMEM((2, 3, MSG2, C), bf16),
            pltpu.VMEM((2, 3, MSG2, C), bf16),
            pltpu.VMEM((2, WIN2, C), f32),
            dma((4 + NG,)), dma((NG, 10)), dma((NG, 10)), dma((7,)), dma((7,)), dma((7,)), dma((7,)),
            dma((NCH, 18)), dma((NCH, 18)), dma((NCH, 24)), dma((NCH,)),
        ],
        compiler_params=pltpu.CompilerParams(
            collective_id=0, has_side_effects=True, vmem_limit_bytes=56 * 1024 * 1024
        ),
        name="resblock_backward",
    )(
        inputs.reshape(OWN, C),
        cotangent.reshape(OWN, C),
        weight.reshape(27, C, C),
        gain,
        shift_term,
    )
    ig, fin = (pltpu.with_memory_space_constraint(v, pltpu.VMEM) for v in (ig, fin))
    ig, wg = pl.pallas_call(
        write_out,
        out_shape=(
            jax.ShapeDtypeStruct((OWN, C), bf16),
            jax.ShapeDtypeStruct((81, C), f32),
        ),
        in_specs=[vmem, vmem],
        out_specs=(hbm, vmem),
        scratch_shapes=[dma],
        name="write_out",
    )(ig, fin)
    return ig.reshape(1, 2, 1, 128, C), wg


def solution(mesh):
    return jax.shard_map(
        per_device,
        mesh=mesh,
        in_specs=(
            P("clip", "tm", "rows", None, None),
            P("clip", "tm", "rows", None, None),
            P(),
            P(),
            P(),
        ),
        out_specs=(P("clip", "tm", "rows", None, None), P(("clip", "tm", "rows"), None)),
        check_vma=False,
    )
```

```python
import jax
import jax.numpy as jnp
from jax import lax
from jax.experimental import pallas as pl
from jax.experimental.pallas import tpu as pltpu
from jax.sharding import PartitionSpec as P

MESH = pl.DeviceIdType.MESH
C = 384
SL = 48
PG = 12
POS = 1024
OWN = 256
EPS = 1e-05
CELLS = 12 * 2048
SCALE = 1.0 / 128
ODD = (1, 7, 13, 21, 9, 15, 23, 3, 11, 17, 5, 19, 25)
ORDER = tuple(range(0, 27, 2)) + ODD
WIN1, CUT1 = 168, 88
BASES, HOPS = (0, 672), (168, 152)
WIN2, HOP2 = 48, 40
GCH = ((0, 384),)
NG = len(GCH)
CH = ((0, 384),)
NCH = len(CH)


MSG = 96
MSG2 = 64
SPAN = 125.0


def encode(values, size):
    n, w = values.shape
    tiles = values.reshape(n // 8, 8, w)
    top = jnp.max(jnp.abs(tiles), axis=0) * 1.01 + 1e-30
    top = top.astype(jnp.bfloat16).astype(jnp.float32)
    code = jnp.exp2(tiles * (SPAN / top)[None]).reshape(n, w)
    return jnp.concatenate([code] + [top] * ((size - n) // 8), 0).astype(jnp.bfloat16)


def decode(message, n):
    wide = message.astype(jnp.float32)
    top = wide[n:n + 8] * (1.0 / SPAN)
    w = wide.shape[1]
    return (jnp.log2(wide[0:n]).reshape(n // 8, 8, w) * top[None]).reshape(n, w)


def kernel(
    x_hbm, cot_hbm, w_hbm, gain_ref, shift_ref, ig_ref, fin,
    x_own, x_send, x_all, cot, wv, gb, stat, normed_s, dsil_s, lcat, prod, part,
    ig_send, ig_recv, out_b, in_b, res1, fout_b, fin_b, res2,
    loc_sem, cs_send, cs_recv, xs_send, xs_recv, is_send, is_recv, r_send, r_recv, f_send, f_recv,
):
    clip, tm, rows = lax.axis_index("clip"), lax.axis_index("tm"), lax.axis_index("rows")
    x_hi, core = tm // 2, tm % 2
    j = tm * 2 + rows
    yy, zz = clip // 4, clip % 4

    def dev(tm_, rows_):
        return (clip, tm_, rows_)

    def ring(tm_, rows_, step):
        hi, co = tm_ // 2, tm_ % 2
        x = (hi * 2 + rows_ + step + 4) % 4
        return (x // 2) * 2 + co, x % 2

    rt, rr = ring(tm, rows, 1)
    lt, lr = ring(tm, rows, -1)
    ot, orow = ring(tm, rows, 2)
    sib_tm = x_hi * 2 + (1 - core)

    yp, ym = ((yy + 1) % 4) * 4 + zz, ((yy + 3) % 4) * 4 + zz
    yo, zo = ((yy + 2) % 4) * 4 + zz, yy * 4 + (zz + 2) % 4
    zp, zm = yy * 4 + (zz + 1) % 4, yy * 4 + (zz + 3) % 4
    barrier = pltpu.get_barrier_semaphore()
    for k in range(1, 8):
        p = (j + k) % 8
        pl.semaphore_signal(barrier, inc=1, device_id=dev(p // 2, p % 2), device_id_type=MESH)
    for other in (yp, ym, zp, zm):
        pl.semaphore_signal(barrier, inc=1, device_id=(other, tm, rows), device_id_type=MESH)


    x_in = pltpu.make_async_copy(x_hbm, x_own, loc_sem.at[0])
    x_in.start()
    own_slot = pl.ds(pl.multiple_of(tm * OWN, OWN), OWN)
    c_in = []
    for c in range(NG):
        copy = pltpu.make_async_copy(
            cot_hbm.at[:, pl.ds(*GCH[c])], cot.at[rows, own_slot, pl.ds(*GCH[c])], loc_sem.at[4 + c]
        )
        copy.start()
        c_in.append(copy)
    w_in = pltpu.make_async_copy(
        w_hbm.at[:, pl.ds(pl.multiple_of(j * SL, SL), SL)], wv, loc_sem.at[2]
    )
    w_in.start()

    pl.semaphore_wait(barrier, 11)

    def frame(tm_, f):
        return pl.ds(pl.multiple_of(tm_ * OWN + f * 128, 128), 128)

    def cot_copy(ch, slot, where, to):
        ref = cot.at[where[0], where[1], pl.ds(*GCH[ch])]
        return pltpu.make_async_remote_copy(
            src_ref=ref, dst_ref=ref,
            send_sem=cs_send.at[ch, slot], recv_sem=cs_recv.at[ch, slot],
            device_id=dev(*to), device_id_type=MESH,
        )

    right, left, sib = (rt, rr), (lt, lr), (sib_tm, rows)
    sends = []

    def send(ch, slot, where, to):
        copy = cot_copy(ch, slot, where, to)
        copy.start()
        sends.append(copy)

    def arrived(ch, slot, where):
        cot_copy(ch, slot, where, right).wait_recv()

    def whole(who):
        return who[1], pl.ds(pl.multiple_of(who[0] * OWN, OWN), OWN)

    def sib_of(who):
        return whole((who[0] + 1 - 2 * (who[0] % 2), who[1]))

    def own(ch):
        c_in[ch].wait()
        send(ch, 0, (rows, frame(tm, 0)), right)
        send(ch, 2, (rows, frame(tm, 1)), left)

    def own_rest(ch):
        send(ch, 1, (rows, frame(tm, 1)), right)
        send(ch, 3, (rows, frame(tm, 0)), left)
        send(ch, 4, (rows, own_slot), sib)

    def fwd1(ch):
        arrived(ch, 0, (lr, frame(lt, 0)))
        send(ch, 5, (lr, frame(lt, 0)), right)
        arrived(ch, 2, (rr, frame(rt, 1)))
        send(ch, 6, (rr, frame(rt, 1)), left)

    def fwd2(ch):
        arrived(ch, 1, (lr, frame(lt, 1)))
        send(ch, 7, whole((lt, lr)), sib)
        arrived(ch, 3, (rr, frame(rt, 0)))
        send(ch, 8, whole((rt, rr)), sib)

    def fwd3(ch):
        arrived(ch, 5, (orow, frame(ot, 0)))
        arrived(ch, 6, (orow, frame(ot, 1)))
        send(ch, 9, whole((ot, orow)), sib)

    def gathered_near(ch):
        arrived(ch, 4, sib_of((tm, rows)))
        arrived(ch, 7, sib_of((lt, lr)))
        arrived(ch, 8, sib_of((rt, rr)))

    def gathered_far(ch):
        arrived(ch, 9, sib_of((ot, orow)))

    own(0)

    x_in.wait()
    x_send[...] = x_own[...].astype(jnp.float32).T.astype(jnp.bfloat16)
    own_lanes = pl.ds(pl.multiple_of(rows * POS + tm * OWN, OWN), OWN)
    x_self = pltpu.make_async_copy(
        x_send.at[pl.ds(pl.multiple_of(j * SL, SL), SL)], x_all.at[:, own_lanes], loc_sem.at[3]
    )
    x_self.start()
    xs = []
    for k in range(1, 8):
        p = (j + k) % 8
        c = pltpu.make_async_remote_copy(
            src_ref=x_send.at[pl.ds(pl.multiple_of(p * SL, SL), SL)], dst_ref=x_all.at[:, own_lanes],
            send_sem=xs_send.at[k - 1], recv_sem=xs_recv.at[k - 1],
            device_id=dev(p // 2, p % 2), device_id_type=MESH,
        )
        c.start()
        xs.append(c)

    own_rest(0)

    gb[0] = jnp.broadcast_to(gain_ref[...].reshape(1, C), (128, C)).T
    gb[1] = jnp.broadcast_to(shift_ref[...].reshape(1, C), (128, C)).T
    for h in range(2):
        cot[h, POS:, :] = jnp.zeros((OWN, C), jnp.bfloat16)
    mine = pl.ds(pl.multiple_of(j * SL, SL), SL)
    gain_l, shift_l = gb[0, mine, :], gb[1, mine, :]

    fwd1(0)

    me = clip * 8 + j
    jobs = []
    for a in range(2):
        far, near = ((yy, zz), (zz, yy))[a]
        again = []
        for i in range(6):
            loc = (21, 19)[a] * far + 5 * near + i
            n = loc // 6
            tap = 2 * n if a == 0 else sum(jnp.where(n == k, t, 0) for k, t in enumerate(ODD))
            r = loc % 6
            tile = tap * 48 + 6 * j + r
            c_to, u = tile // 81, tile % 81
            j_to = jnp.minimum(u // 10, 7)
            if i < 4:
                ok = jnp.bool_(True)
            elif a == 0:
                ok = jnp.logical_or(i < 5, near == 3)
            elif i == 4:
                ok = jnp.logical_or(near < 3, far == 3)
            else:
                ok = jnp.logical_and(near == 3, far == 3)
            jobs.append((ok, c_to * 8 + j_to, u - 10 * j_to))
            edge = jnp.logical_and(u - 10 * j_to == 0, j_to > 0)
            again.append((jnp.logical_and(ok, edge), c_to * 8 + jnp.maximum(j_to - 1, 0), 10))
        jobs += again

    x_self.wait()
    for c in xs:
        c.wait_recv()

    row_g = lax.broadcasted_iota(jnp.int32, (SL, SL), 0)
    col_g = lax.broadcasted_iota(jnp.int32, (SL, SL), 1)

    def group_of(i):
        return sum((i >= PG * k).astype(jnp.int32) for k in (1, 2, 3))

    same = (group_of(row_g) == group_of(col_g)).astype(jnp.float32)

    def group_mean(values):
        total = jnp.sum(values, axis=1, keepdims=True)
        return jnp.dot(
            same, jnp.broadcast_to(total, (SL, 128)), precision=lax.Precision.HIGHEST,
            preferred_element_type=jnp.float32,
        ) * (1.0 / CELLS)

    s1 = jnp.zeros((SL, 128), jnp.float32)
    s2 = jnp.zeros((SL, 128), jnp.float32)
    for b in range(16):
        v = x_all[:, b * 128:(b + 1) * 128].astype(jnp.float32)
        s1 = s1 + v
        s2 = s2 + v * v
    mean = group_mean(s1)
    rstd = lax.rsqrt(group_mean(s2) - mean * mean + EPS)
    stat[...] = rstd

    lane = lax.broadcasted_iota(jnp.int32, (SL, 128), 1)
    for h in range(2):
        for dt in range(2):
            for dw in range(3):
                r0 = h * 432 + (dt * 3 + dw) * SL
                lcat[r0:r0 + SL, 0:(2 - dt) * 128] = jnp.zeros((SL, (2 - dt) * 128), jnp.bfloat16)
        for t in range(8):
            b = h * 8 + t
            sl = slice(b * 128, (b + 1) * 128)
            v = x_all[:, sl].astype(jnp.float32)
            normed = (v - mean) * rstd
            pre = normed * gain_l + shift_l
            s = 1.0 / (1.0 + jnp.exp(-pre))
            act = pre * s
            normed_s[:, sl] = normed
            dsil_s[:, sl] = s * (1.0 + pre * (1.0 - s)) * gain_l
            before = jnp.where(lane == 0, 0.0, pltpu.roll(act, 1, 1))
            after = jnp.where(lane == 127, 0.0, pltpu.roll(act, 127, 1))
            for dw, a in ((0, before), (1, act), (2, after)):
                a = a.astype(jnp.bfloat16)
                for dt in range(3):
                    t_out = t + 2 - dt
                    if t_out < 8:
                        r0 = h * 432 + (dt * 3 + dw) * SL
                        lcat[r0:r0 + SL, t_out * 128:(t_out + 1) * 128] = a

    half = POS // 2
    near_k = pl.ds(pl.multiple_of(x_hi * half, half), half)
    far_k = pl.ds(pl.multiple_of((1 - x_hi) * half, half), half)

    def weight_grad_near():
        prod[1 - rows] = jnp.dot(lcat[...], cot[1 - rows, 0:POS, :], preferred_element_type=jnp.float32)

    def weight_grad_far():
        prod[rows] = jnp.dot(lcat[:, near_k], cot[rows, near_k, :], preferred_element_type=jnp.float32)
        gathered_far(0)
        prod[rows] += jnp.dot(lcat[:, far_k], cot[rows, far_k, :], preferred_element_type=jnp.float32)
        for dt in range(3):
            for dw in range(3):
                q = (dt * 3 + dw) * SL
                near = [prod[r, k:k + SL] for r in range(2) for k in (q, q + 432)]
                for dh, v in ((0, near[2]), (1, near[0] + near[3]), (2, near[1])):
                    r0 = ORDER.index(dt * 9 + dh * 3 + dw) * SL
                    part[r0:r0 + SL] = v

    def ring_copy(ch, slot, src, dst, to):
        return pltpu.make_async_remote_copy(
            src_ref=src, dst_ref=dst, send_sem=r_send.at[ch, slot], recv_sem=r_recv.at[ch, slot],
            device_id=(to, tm, rows), device_id_type=MESH,
        )

    class Ring:
        def __init__(self, ch, slot, src, base, hop, pos, plus, minus, out_b, in_b, out):
            self.src, self.out, self.out_b, self.in_b = src, out, out_b, in_b

            def at(k, lo, hi):
                return pl.ds(pl.multiple_of(base + ((pos + k) % 4) * hop + lo, 8), hi - lo)

            self.at = at
            self.all = [
                ring_copy(ch, slot + k, out_b.at[k], in_b.at[k], minus if k % 2 else plus) for k in range(6)
            ]

        def put(self, k, values):
            self.out_b[k] = encode(values, MSG)
            self.all[k].start()

        def got(self, k, n):
            self.all[k].wait_recv()
            return decode(self.in_b[k], n)

        def start(self):
            self.put(0, self.src[self.at(2, 0, CUT1), :])
            self.put(1, self.src[self.at(2, CUT1, WIN1), :])

        def near(self):
            self.put(2, self.src[self.at(1, CUT1, WIN1), :])
            self.put(3, self.src[self.at(3, 0, CUT1), :])

        def middle(self):
            self.put(4, self.got(0, CUT1) + self.src[self.at(1, 0, CUT1), :])
            self.put(5, self.got(1, WIN1 - CUT1) + self.src[self.at(3, CUT1, WIN1), :])

        def end(self):
            self.out[0:CUT1] = self.src[self.at(0, 0, CUT1), :] + self.got(3, CUT1) + self.got(4, CUT1)
            self.out[CUT1:WIN1] = (
                self.src[self.at(0, CUT1, WIN1), :] + self.got(2, WIN1 - CUT1) + self.got(5, WIN1 - CUT1)
            )

    class Direct:
        def __init__(self, ch, slot, src, pos, to, out_b, in_b, out):
            self.src, self.out_b, self.in_b, self.out = src, out_b, in_b, out
            self.at = [pl.ds(pl.multiple_of(((pos + k) % 4) * HOP2, 8), WIN2) for k in range(4)]
            self.all = [ring_copy(ch, slot + k, out_b.at[k], in_b.at[k], to[k]) for k in range(3)]

        def start(self):
            for k in (1, 0, 2):
                self.out_b[k] = encode(self.src[self.at[k + 1], :], MSG2)
                self.all[k].start()

        def end(self):
            total = self.src[self.at[0], :]
            for k in (0, 2, 1):
                self.all[k].wait_recv()
                total = total + decode(self.in_b[k], WIN2)
            self.out[...] = total

    first, second = [], []
    for c in range(NCH):
        for a in range(2):
            lanes = pl.ds(*CH[c])
            along = ((yy, yp, ym, yo), (zz, zp, zm, zo))
            pos1, plus1, minus1, _ = along[a]
            pos2, plus2, minus2, far2 = along[1 - a]
            first.append(Ring(
                c, a * 6, part.at[:, lanes], BASES[a], HOPS[a], pos1, plus1, minus1,
                out_b.at[a, :, :, lanes], in_b.at[a, :, :, lanes], res1.at[a, :, lanes],
            ))
            second.append(Direct(
                c, 12 + a * 3, res1.at[a, :, lanes], pos2, (plus2, far2, minus2),
                fout_b.at[a, :, :, lanes], fin_b.at[a, :, :, lanes], res2.at[a, :, lanes],
            ))

    def start1(ch):
        for st in first[2 * ch:2 * ch + 2]:
            st.start()

    def near1(ch):
        for st in first[2 * ch:2 * ch + 2]:
            st.near()

    def mid1(ch):
        for st in first[2 * ch:2 * ch + 2]:
            st.middle()

    def turn(ch):
        for st, nxt in zip(first[2 * ch:2 * ch + 2], second[2 * ch:2 * ch + 2]):
            st.end()
            nxt.start()

    def end2(ch):
        for a in range(2):
            second[2 * ch + a].end()
            scatter(ch, begin, a * 12, a * 12 + 12)

    nt = (((1,), (1,)), ((), ()))
    grads, cots = [], []

    def grad_active(h):
        acc = jnp.zeros((144, POS), jnp.float32)
        for hs in range(2):
            dh = h - hs + 1
            for dt in range(3):
                tap = dt * 9 + dh * 3
                w_rows = wv[tap:tap + 3].reshape(144, C)
                c_rows = cot[hs, (2 - dt) * 128:(2 - dt) * 128 + POS, :]
                if hs == h and dt == 2:
                    both = lax.dot_general(
                        jnp.concatenate([w_rows, pick], 0), c_rows, nt, preferred_element_type=jnp.float32
                    )
                    cots.append(both[144:192])
                    acc = acc + both[0:144]
                else:
                    acc = acc + lax.dot_general(w_rows, c_rows, nt, preferred_element_type=jnp.float32)
        grads.append(acc)

    def input_grad():
        t1 = jnp.zeros((SL, 128), jnp.float32)
        t2 = jnp.zeros((SL, 128), jnp.float32)
        for h in range(2):
            for t in range(8):
                sl = slice(t * 128, (t + 1) * 128)
                gl = slice((h * 8 + t) * 128, (h * 8 + t + 1) * 128)
                g0, g1, g2 = (grads[h][k * SL:(k + 1) * SL, sl] for k in range(3))
                g = (
                    g1
                    + jnp.where(lane == 127, 0.0, pltpu.roll(g0, 127, 1))
                    + jnp.where(lane == 0, 0.0, pltpu.roll(g2, 1, 1))
                )
                gn = g * dsil_s[:, gl]
                dsil_s[:, gl] = gn
                t1 = t1 + gn
                t2 = t2 + gn * normed_s[:, gl]
        m1, m2 = group_mean(t1), group_mean(t2)
        rstd_l = stat[...]
        for h in range(2):
            for t in range(8):
                sl = slice(t * 128, (t + 1) * 128)
                gl = slice((h * 8 + t) * 128, (h * 8 + t + 1) * 128)
                out = cots[h][:, sl] + rstd_l * (dsil_s[:, gl] - m1 - normed_s[:, gl] * m2)
                ig_send[:, gl] = out.astype(jnp.bfloat16)

    ig_self = pltpu.make_async_copy(ig_send.at[:, own_lanes], ig_recv.at[mine], loc_sem.at[3])
    igs = []
    for k in range(1, 8):
        p = (j + k) % 8
        lanes = pl.ds(pl.multiple_of((p % 2) * POS + (p // 2) * OWN, OWN), OWN)
        igs.append(pltpu.make_async_remote_copy(
            src_ref=ig_send.at[:, lanes], dst_ref=ig_recv.at[mine],
            send_sem=is_send.at[k - 1], recv_sem=is_recv.at[k - 1],
            device_id=dev(p // 2, p % 2), device_id_type=MESH,
        ))

    def ig_out():
        ig_self.wait()
        for c in igs:
            c.wait_recv()
        ig_ref[...] = ig_recv[...].astype(jnp.float32).T.astype(jnp.bfloat16)

    def scatter(ch, act, lo=0, hi=24):
        for n in range(lo, hi):
            ok, d_to, slot = jobs[n]
            src = res2.at[n // 12, pl.ds(n % 6 * 8, 8), pl.ds(*CH[ch])]
            act(ch, n, ok, src, d_to, slot)

    def fin_at(ch, slot):
        return fin.at[pl.ds(pl.multiple_of(slot * 8, 8), 8), pl.ds(*CH[ch])]

    def fin_copy(ch, n, src, d_to, slot):
        return pltpu.make_async_remote_copy(
            src_ref=src, dst_ref=fin_at(ch, slot), send_sem=f_send.at[ch, n], recv_sem=f_recv.at[ch],
            device_id=(d_to // 8, d_to % 8 // 2, d_to % 2), device_id_type=MESH,
        )

    def begin(ch, n, ok, src, d_to, slot):
        @pl.when(jnp.logical_and(ok, d_to == me))
        def _():
            pltpu.make_async_copy(src, fin_at(ch, slot), f_recv.at[ch]).start()

        @pl.when(jnp.logical_and(ok, d_to != me))
        def _():
            fin_copy(ch, n, src, d_to, slot).start()

    def finish(ch, n, ok, src, d_to, slot):
        @pl.when(jnp.logical_and(ok, d_to != me))
        def _():
            fin_copy(ch, n, src, d_to, slot).wait_send()

    fwd2(0)
    gathered_near(0)
    weight_grad_near()
    fwd3(0)
    weight_grad_far()
    start1(0)
    near1(0)
    w_in.wait()
    pick = (
        lax.broadcasted_iota(jnp.int32, (SL, C), 1)
        == lax.broadcasted_iota(jnp.int32, (SL, C), 0) + j * SL
    ).astype(jnp.bfloat16)
    grad_active(0)
    grad_active(1)
    mid1(0)
    input_grad()
    for c in [ig_self] + igs:
        c.start()
    turn(0)
    end2(0)
    ig_out()

    for c in sends + xs + igs:
        c.wait_send()
    for st in first + second:
        for c in st.all:
            c.wait_send()
    for c in range(NCH):
        scatter(c, finish)
    for c in range(NCH):
        lanes = fin.at[:, pl.ds(*CH[c])]
        pltpu.make_async_copy(lanes, lanes, f_recv.at[c]).wait()


def write_out(ig_in, fin, ig_out, wg_out, sem):
    copy = pltpu.make_async_copy(ig_in, ig_out, sem)
    copy.start()
    j = lax.axis_index("tm") * 2 + lax.axis_index("rows")
    for k in range(8):
        @pl.when(j == k)
        def _(k=k):
            wg_out[...] = fin[k:k + 81, :] * SCALE
    copy.wait()


def per_device(inputs, cotangent, weight, gain, shift_term):
    f32, bf16 = jnp.float32, jnp.bfloat16
    hbm = pl.BlockSpec(memory_space=pltpu.HBM)
    vmem = pl.BlockSpec(memory_space=pltpu.VMEM)
    dma = pltpu.SemaphoreType.DMA
    ig, fin = pl.pallas_call(
        kernel,
        out_shape=(pltpu.VMEM((OWN, C), bf16), pltpu.VMEM((88, C), f32)),
        in_specs=[hbm, hbm, hbm, vmem, vmem],
        out_specs=(vmem, vmem),
        scratch_shapes=[
            pltpu.VMEM((OWN, C), bf16),
            pltpu.VMEM((C, OWN), bf16),
            pltpu.VMEM((SL, 2 * POS), bf16),
            pltpu.VMEM((2, POS + OWN, C), bf16),
            pltpu.VMEM((27, SL, C), bf16),
            pltpu.VMEM((2, C, 128), f32),
            pltpu.VMEM((SL, 128), f32),
            pltpu.VMEM((SL, 2 * POS), f32),
            pltpu.VMEM((SL, 2 * POS), f32),
            pltpu.VMEM((864, POS), bf16),
            pltpu.VMEM((2, 864, C), f32),
            pltpu.VMEM((1296, C), f32),
            pltpu.VMEM((SL, 2 * POS), bf16),
            pltpu.VMEM((C, OWN), bf16),
            pltpu.VMEM((2, 6, MSG, C), bf16),
            pltpu.VMEM((2, 6, MSG, C), bf16),
            pltpu.VMEM((2, WIN1, C), f32),
            pltpu.VMEM((2, 3, MSG2, C), bf16),
            pltpu.VMEM((2, 3, MSG2, C), bf16),
            pltpu.VMEM((2, WIN2, C), f32),
            dma((4 + NG,)), dma((NG, 10)), dma((NG, 10)), dma((7,)), dma((7,)), dma((7,)), dma((7,)),
            dma((NCH, 18)), dma((NCH, 18)), dma((NCH, 24)), dma((NCH,)),
        ],
        compiler_params=pltpu.CompilerParams(
            collective_id=0, has_side_effects=True, vmem_limit_bytes=56 * 1024 * 1024
        ),
        name="resblock_backward",
    )(
        inputs.reshape(OWN, C),
        cotangent.reshape(OWN, C),
        weight.reshape(27, C, C),
        gain,
        shift_term,
    )
    ig, fin = (pltpu.with_memory_space_constraint(v, pltpu.VMEM) for v in (ig, fin))
    ig, wg = pl.pallas_call(
        write_out,
        out_shape=(
            jax.ShapeDtypeStruct((OWN, C), bf16),
            jax.ShapeDtypeStruct((81, C), f32),
        ),
        in_specs=[vmem, vmem],
        out_specs=(hbm, vmem),
        scratch_shapes=[dma],
        name="write_out",
    )(ig, fin)
    return ig.reshape(1, 2, 1, 128, C), wg


def solution(mesh):
    return jax.shard_map(
        per_device,
        mesh=mesh,
        in_specs=(
            P("clip", "tm", "rows", None, None),
            P("clip", "tm", "rows", None, None),
            P(),
            P(),
            P(),
        ),
        out_specs=(P("clip", "tm", "rows", None, None), P(("clip", "tm", "rows"), None)),
        check_vma=False,
    )
```
